32 devices in a mesh: lat: 4 (over y, core), lon: 2 (over x), dep: 4 (over z).
Axes of the slice: x: 2, y: 2, z: 4, core: 2. Of those that a mesh axis runs over, the one named last changes fastest.
Arguments:
- thick: float32 [16, 32, 256], P('dep', 'lat', 'lon'), may hold values from 0.5 to 2
- zonal: float32 [16, 32, 256], P('dep', 'lat', 'lon'), may hold values from -6 to 6
- merid: float32 [16, 32, 256], P('dep', 'lat', 'lon'), may hold values from -6 to 6
- d_zonal: bfloat16 [64, 16, 32, 256], P(None, 'dep', 'lat', 'lon'), may hold values from -6 to 6
- d_merid: bfloat16 [64, 16, 32, 256], P(None, 'dep', 'lat', 'lon'), may hold values from -6 to 6
- d_thick: bfloat16 [64, 16, 32, 256], P(None, 'dep', 'lat', 'lon'), may hold values from -6 to 6
- land_sea: int32 [16, 32, 256], P('dep', 'lat', 'lon'), may hold values 0 or 1
- line_label: int32 [32, 256], P('lat', 'lon'), may hold values from 0 to 32
- island_label: int32 [32, 256], P('lat', 'lon'), may hold values from 0 to 32
Outputs:
- stream: float32 [64, 32, 256], P('dep', 'lat', 'lon')
The draws below stay inside these ranges and needn't reach their ends.
All inputs are finite; a program needn't handle non-finite values. No bound on the sum of `land_sea` on one device may be relied on, other than what follows from the above.
Results may differ from the reference program's by a relative error of at most 0.0003.
Values sent between devices are 32-bit elements; how exact they have to be, the bound alone decides.
No kernel may reach another device: no remote copies, remote signals or barrier semaphores. Data moves between devices by JAX's collectives and lax.ppermute only.
A program may use at most 64 MiB of HBM per device.

```python
import math
import jax
import jax.numpy as jnp
from jax import lax

DIR = 64
NISL = 32
NLAT = 32
NLON = 256
NDEP = 16


def plant(entries, key, smallest, largest):
    longest = entries.shape.index(max(entries.shape))
    spots = []
    for shift in (0, 1):
        where = [jax.random.randint(jax.random.fold_in(key, axis), (), 0, length) for axis, length in enumerate(entries.shape)]
        where[longest] = (where[longest] + shift) % entries.shape[longest]
        spots.append(tuple(where))
    return entries.at[spots[0]].set(smallest).at[spots[1]].set(largest)


def block_levels(stream_key, extent, shards, low, high):
    def one(axis_at, shards_of):
        draws = jax.random.uniform(jax.random.fold_in(jax.random.fold_in(stream_key, 6), axis_at), (shards_of,), jnp.float32, low / len(shards), high / len(shards))
        return jnp.repeat(jnp.exp(draws), extent[axis_at] // shards_of).reshape((-1,) + (1,) * (len(extent) - axis_at - 1))

    level = one(*shards[0])
    for cut in shards[1:]:
        level = level * one(*cut)
    return level


def scatter_about(key, shape, deviation, limit, cuts=(), kind=jnp.bfloat16):
    gain = block_levels(key, shape, cuts, -0.22, 0.18) if cuts else 1.0
    values = jax.random.normal(key, shape, jnp.float32) * deviation * gain
    return jnp.minimum(jnp.maximum(values, -limit), limit).astype(kind)


def setup_inputs(seed: int = 0) -> dict:
    streams_of = jax.random.split(jax.random.key(seed), 10)
    thick = jnp.clip(jnp.exp(math.log(2.0) - 1.3862944 * jax.random.uniform(streams_of[0], (NDEP, NLAT, NLON), jnp.float32) ** block_levels(streams_of[0], (NDEP, NLAT, NLON), ((0, 4), (1, 4), (2, 2)), -0.2, 0.2)), 0.5, 2.0)
    zonal = scatter_about(streams_of[1], (NDEP, NLAT, NLON), 1.0, 6.0, ((0, 4), (1, 4), (2, 2)), jnp.float32)
    merid = scatter_about(streams_of[2], (NDEP, NLAT, NLON), 1.0, 6.0, ((0, 4), (1, 4), (2, 2)), jnp.float32)
    d_zonal = scatter_about(streams_of[3], (DIR, NDEP, NLAT, NLON), 1.0, 6.0, ((1, 4), (2, 4), (3, 2)))
    d_merid = scatter_about(streams_of[4], (DIR, NDEP, NLAT, NLON), 1.0, 6.0, ((1, 4), (2, 4), (3, 2)))
    d_thick = scatter_about(streams_of[5], (DIR, NDEP, NLAT, NLON), 1.0, 6.0, ((1, 4), (2, 4), (3, 2)))
    land_sea = plant((jax.random.randint(streams_of[6], (NDEP, NLAT, NLON), 0, 4) < 3).astype(jnp.int32), jax.random.fold_in(streams_of[6], 1), 0, 1)
    line_label = plant(jax.random.randint(streams_of[7], (NLAT, NLON), 0, NISL + 1), jax.random.fold_in(streams_of[7], 1), 0, NISL).astype(jnp.int32)
    island_label = plant(jax.random.randint(streams_of[8], (NLAT, NLON), 0, NISL + 1), jax.random.fold_in(streams_of[8], 1), 0, NISL).astype(jnp.int32)
    return dict(thick=thick, zonal=zonal, merid=merid, d_zonal=d_zonal, d_merid=d_merid, d_thick=d_thick, land_sea=land_sea, line_label=line_label, island_label=island_label)


def reference(thick, zonal, merid, d_zonal, d_merid, d_thick, land_sea, line_label, island_label):
    sea = land_sea.astype(jnp.float32)
    level_scale = 1.0 / math.sqrt(NDEP)
    east_thick = sea * thick
    east_base = sea * zonal
    north_base = sea * merid

    def one_direction(pieces):
        dz, dm, dt = pieces
        dz = dz.astype(jnp.float32)
        dm = dm.astype(jnp.float32)
        dt = dt.astype(jnp.float32)
        east = lax.optimization_barrier(jnp.sum(east_thick * dz + dt * east_base, axis=0)) * level_scale
        north = lax.optimization_barrier(jnp.sum(east_thick * dm + dt * north_base, axis=0)) * level_scale
        return (east, north)
    east, north = lax.map(one_direction, (d_zonal, d_merid, d_thick))
    psi = -jnp.cumsum(east, axis=1) * (1.0 / math.sqrt(NLAT))
    labels = jnp.arange(1, NISL + 1, dtype=jnp.int32)
    line_hot = (line_label[None] == labels[:, None, None]).astype(jnp.float32)
    island_hot = (island_label[None] == labels[:, None, None]).astype(jnp.float32)
    circ = jnp.einsum('dij,mij->dm', north, line_hot, precision=lax.Precision.HIGHEST)
    circ = circ * (1.0 / math.sqrt(NLAT * NLON / (NISL + 1)))
    return psi + jnp.einsum('dm,mij->dij', circ, island_hot, precision=lax.Precision.HIGHEST)
```

```python
import math

import jax
import jax.numpy as jnp
from jax import lax
from jax.sharding import PartitionSpec as P

NISL = 32


def shards(thick, zonal, merid, d_zonal, d_merid, d_thick, land_sea, line_label, island_label):
    dirs, levels, rows, cols = d_zonal.shape
    n_lat = lax.axis_size("lat")
    n_lon = lax.axis_size("lon")
    n_dep = lax.axis_size("dep")
    me = lax.axis_index("dep")
    share = dirs // n_dep
    level_scale = 1.0 / math.sqrt(levels * n_dep)
    row_scale = 1.0 / math.sqrt(rows * n_lat)
    line_scale = 1.0 / math.sqrt(rows * n_lat * cols * n_lon / (NISL + 1))
    sea = land_sea.astype(jnp.float32)
    east_thick = sea * thick
    east_part = jnp.sum(
        east_thick[None] * d_zonal.astype(jnp.float32)
        + d_thick.astype(jnp.float32) * (sea * zonal)[None],
        axis=1,
    ) * (-level_scale * row_scale)
    blocks = east_part.reshape(n_dep, share, rows, cols)
    arrived = [lax.dynamic_index_in_dim(blocks, me, 0, keepdims=False)]
    for shift in range(1, n_dep):
        block = lax.dynamic_index_in_dim(blocks, (me + shift) % n_dep, 0, keepdims=False)
        arrived.append(
            lax.ppermute(block, "dep", [(i, (i + shift) % n_dep) for i in range(n_dep)])
        )
    north_part = jnp.sum(
        east_thick[None] * d_merid.astype(jnp.float32)
        + d_thick.astype(jnp.float32) * (sea * merid)[None],
        axis=1,
    ) * (level_scale * line_scale)
    labels = jnp.arange(1, NISL + 1, dtype=jnp.int32)
    line_hot = (line_label[None] == labels[:, None, None]).astype(jnp.float32)
    island_hot = (island_label[None] == labels[:, None, None]).astype(jnp.float32)
    local_circ = jnp.einsum("dij,mij->dm", north_part, line_hot, precision=lax.Precision.HIGHEST)
    totals = jnp.sum(east_part, axis=1)
    small = jnp.concatenate(
        [totals, jnp.pad(local_circ, ((0, 0), (0, cols - NISL)))], axis=1
    ).reshape(n_dep, share, 2 * cols)
    small = jnp.sum(lax.all_to_all(small, "dep", 0, 0), axis=0)
    every = lax.all_gather(small, ("lat", "lon")).reshape(n_lat, n_lon, share, 2 * cols)
    circ = jnp.sum(every[..., cols : cols + NISL], axis=(0, 1))
    mine = lax.axis_index("lat")
    of_lon = lax.dynamic_index_in_dim(every, lax.axis_index("lon"), 1, keepdims=False)
    south = (jnp.arange(n_lat) < mine).astype(jnp.float32)
    before = jnp.sum(of_lon[..., :cols] * south[:, None, None], axis=0)
    east_own = sum(arrived[1:], arrived[0])
    psi = jnp.cumsum(east_own, axis=1) + before[:, None, :]
    return psi + jnp.einsum("dm,mij->dij", circ, island_hot, precision=lax.Precision.HIGHEST)


def solution(mesh):
    return jax.shard_map(
        shards,
        mesh=mesh,
        in_specs=(
            P("dep", "lat", "lon"),
            P("dep", "lat", "lon"),
            P("dep", "lat", "lon"),
            P(None, "dep", "lat", "lon"),
            P(None, "dep", "lat", "lon"),
            P(None, "dep", "lat", "lon"),
            P("dep", "lat", "lon"),
            P("lat", "lon"),
            P("lat", "lon"),
        ),
        out_specs=P("dep", "lat", "lon"),
        check_vma=False,
    )
```

```python
import functools
import math

import jax
import jax.numpy as jnp
from jax import lax
from jax.experimental import pallas as pl
from jax.experimental.pallas import tpu as pltpu
from jax.sharding import PartitionSpec as P

NISL = 32
VMEM_BYTES = 32 * 1024 * 1024


def transport_kernel(
    east_scale, north_scale, thick, zonal, merid, sea, line, dz_hbm, dm_hbm, dt_hbm, out,
    dz, dm, dt, north, sems,
):
    n_dep = out.shape[0]
    share = dz.shape[0] // n_dep
    rows, cols = line.shape
    deep = dz.shape[1]

    def copies(b):
        part = pl.ds(b * share, share)
        return [
            pltpu.make_async_copy(src.at[part], dst.at[part], sems.at[k, b])
            for k, (src, dst) in enumerate(((dz_hbm, dz), (dm_hbm, dm), (dt_hbm, dt)))
        ]

    for b in range(n_dep):
        for copy in copies(b):
            copy.start()
    wet = sea[...].astype(jnp.float32)
    east_thick = wet * thick[...] * east_scale
    east_base = wet * zonal[...] * east_scale
    north_thick = wet * thick[...] * north_scale
    north_base = wet * merid[...] * north_scale
    labels = lax.broadcasted_iota(jnp.int32, (NISL, cols), 0) + 1
    hot = jnp.concatenate(
        [(line[i : i + 1, :] == labels).astype(jnp.bfloat16) for i in range(rows)], axis=0
    )
    hot = jnp.concatenate([hot, hot], axis=1)

    def levels(value):
        return jnp.sum(value.reshape(deep // rows, rows, cols), axis=0)

    group = lax.broadcasted_iota(jnp.int32, (rows, cols), 1) // NISL
    own = lax.broadcasted_iota(jnp.int32, (rows, rows * NISL), 1) // NISL == (
        lax.broadcasted_iota(jnp.int32, (rows, rows * NISL), 0)
    )
    for b in range(n_dep):
        for copy in copies(b):
            copy.wait()
        for d in range(share):
            at = b * share + d
            z, m, t = (ref[at].astype(jnp.float32) for ref in (dz, dm, dt))
            out[b, d * rows : (d + 1) * rows, :] = levels(z * east_thick + t * east_base)
            north[d * rows : (d + 1) * rows, :] = levels(m * north_thick + t * north_base)
        value = north[...]
        high = value.astype(jnp.bfloat16)
        low = (value - high.astype(jnp.float32)).astype(jnp.bfloat16)
        sums = lax.dot_general(
            jnp.concatenate([high, low], axis=1), hot, (((1,), (1,)), ((), ())),
            preferred_element_type=jnp.float32,
        )
        sums = jnp.where(own[None], sums.reshape(share, rows, rows * NISL), 0.0)
        sums = sums[:, :, :cols] + sums[:, :, cols:]
        sums = jnp.sum(sums, axis=1)
        sums = sums + pltpu.roll(sums, cols // 2, 1)
        sums = sums + pltpu.roll(sums, cols // 4, 1)
        first, second = sums[:8], sums[8:]
        packed = jnp.where(
            group < 2,
            jnp.where(group == 0, first, pltpu.roll(first, 4, 0)),
            jnp.where(group == 2, second, pltpu.roll(second, 4, 0)),
        )
        out[b, share * rows :, :] = packed


def prefix_kernel(arrived, psi, out):
    share, rows, cols = psi.shape
    value = arrived[0]
    for b in range(1, arrived.shape[0]):
        value = value + arrived[b]
    running = value[: share * rows].reshape(share, rows, cols)
    row = lax.broadcasted_iota(jnp.int32, (share, rows, cols), 1)
    step = 1
    while step < rows:
        running = running + jnp.where(row >= step, pltpu.roll(running, step, 1), 0.0)
        step *= 2
    psi[...] = running
    totals = running[:, rows - 1, :]
    small = jnp.concatenate([totals, value[share * rows :]], axis=0)
    for p in range(out.shape[0]):
        out[p] = small


def stream_kernel(n_lon, arrived, psi, island, out):
    share, rows, cols = psi.shape
    mine = lax.axis_index("lat")
    lon = lax.axis_index("lon")
    n_lat = arrived.shape[0] // n_lon
    before = jnp.zeros((share, cols), jnp.float32)
    circ = arrived[0, share:, :]
    for p in range(1, arrived.shape[0]):
        circ = circ + arrived[p, share:, :]
    for i in range(n_lat - 1):
        before = before + jnp.where(i < mine, arrived[i * n_lon + lon, :share, :], 0.0)
    label = island[...]
    some = label > 0
    place = jnp.maximum(label - 1, 0)
    for d in range(share):
        g, r = d // 4, d % 4
        constant = jnp.take_along_axis(
            jnp.broadcast_to(circ[r : r + 1, :], (rows, cols)), place + g * NISL, axis=1
        )
        out[d] = psi[d] + before[d : d + 1, :] + jnp.where(some, constant, 0.0)


def shards(thick, zonal, merid, d_zonal, d_merid, d_thick, land_sea, line_label, island_label):
    dirs, levels, rows, cols = d_zonal.shape
    n_lat = lax.axis_size("lat")
    n_lon = lax.axis_size("lon")
    n_dep = lax.axis_size("dep")
    share = dirs // n_dep
    level_scale = 1.0 / math.sqrt(levels * n_dep)
    row_scale = 1.0 / math.sqrt(rows * n_lat)
    line_scale = 1.0 / math.sqrt(rows * n_lat * cols * n_lon / (NISL + 1))
    deep = levels * rows
    base = [x.reshape(deep, cols) for x in (thick, zonal, merid, land_sea)]
    moving = [x.reshape(dirs, deep, cols) for x in (d_zonal, d_merid, d_thick)]
    vmem = pl.BlockSpec(memory_space=pltpu.VMEM)
    hbm = pl.BlockSpec(memory_space=pl.ANY)
    params = pltpu.CompilerParams(vmem_limit_bytes=VMEM_BYTES)
    sent = pl.pallas_call(
        functools.partial(transport_kernel, -level_scale * row_scale, level_scale * line_scale),
        out_shape=jax.ShapeDtypeStruct((n_dep, share * rows + 8, cols), jnp.float32),
        in_specs=[vmem] * 5 + [hbm] * 3,
        out_specs=vmem,
        scratch_shapes=[pltpu.VMEM((dirs, deep, cols), jnp.bfloat16)] * 3
        + [pltpu.VMEM((share * rows, cols), jnp.float32), pltpu.SemaphoreType.DMA((3, n_dep))],
        compiler_params=params,
        name="transport",
    )(*base, line_label, *moving)
    arrived = lax.all_to_all(sent, "dep", 0, 0)
    psi, small = pl.pallas_call(
        prefix_kernel,
        out_shape=(
            jax.ShapeDtypeStruct((share, rows, cols), jnp.float32),
            jax.ShapeDtypeStruct((n_lat * n_lon, share + 8, cols), jnp.float32),
        ),
        in_specs=[vmem],
        out_specs=(vmem, vmem),
        compiler_params=params,
        name="prefix",
    )(arrived)
    small = lax.all_to_all(small, ("lat", "lon"), 0, 0)
    return pl.pallas_call(
        functools.partial(stream_kernel, n_lon),
        out_shape=jax.ShapeDtypeStruct((share, rows, cols), jnp.float32),
        in_specs=[vmem] * 3,
        out_specs=vmem,
        compiler_params=params,
        name="stream",
    )(small, psi, island_label)


def solution(mesh):
    return jax.shard_map(
        shards,
        mesh=mesh,
        in_specs=(
            P("dep", "lat", "lon"),
            P("dep", "lat", "lon"),
            P("dep", "lat", "lon"),
            P(None, "dep", "lat", "lon"),
            P(None, "dep", "lat", "lon"),
            P(None, "dep", "lat", "lon"),
            P("dep", "lat", "lon"),
            P("lat", "lon"),
            P("lat", "lon"),
        ),
        out_specs=P("dep", "lat", "lon"),
        check_vma=False,
    )
```

```python
import functools
import math

import jax
import jax.numpy as jnp
from jax import lax
from jax.experimental import pallas as pl
from jax.experimental.pallas import tpu as pltpu
from jax.sharding import PartitionSpec as P

NISL = 32
VMEM_BYTES = 16 * 1024 * 1024


def transport_kernel(
    east_scale, north_scale, thick_hbm, zonal_hbm, merid_hbm, sea_hbm, line_hbm, dz_hbm, dm_hbm,
    dt_hbm, east, small, thick, zonal, merid, sea, line, dz, dm, dt, north, base_sems, sems,
):
    n_dep = east.shape[0]
    share = dz.shape[0] // n_dep
    rows, cols = line.shape
    deep = dz.shape[1]
    base = [
        pltpu.make_async_copy(src, dst, base_sems.at[k])
        for k, (src, dst) in enumerate(
            (
                (thick_hbm, thick), (zonal_hbm, zonal), (merid_hbm, merid), (sea_hbm, sea),
                (line_hbm, line),
            )
        )
    ]

    def copies(b):
        part = pl.ds(b * share, share)
        return [
            pltpu.make_async_copy(src.at[part], dst.at[part], sems.at[k, b])
            for k, (src, dst) in enumerate(((dz_hbm, dz), (dm_hbm, dm), (dt_hbm, dt)))
        ]

    for copy in base:
        copy.start()
    for b in range(n_dep):
        for copy in copies(b):
            copy.start()
    for copy in base:
        copy.wait()
    wet = sea[...].astype(jnp.float32)
    east_thick = wet * thick[...] * east_scale
    east_base = wet * zonal[...] * east_scale
    north_thick = wet * thick[...] * north_scale
    north_base = wet * merid[...] * north_scale
    labels = lax.broadcasted_iota(jnp.int32, (NISL, cols), 0) + 1
    hot = jnp.concatenate(
        [(line[i : i + 1, :] == labels).astype(jnp.bfloat16) for i in range(rows)], axis=0
    )
    hot = jnp.concatenate([hot, hot], axis=1)

    def levels(value):
        return jnp.sum(value.reshape(deep // rows, rows, cols), axis=0)

    group = lax.broadcasted_iota(jnp.int32, (rows, cols), 1) // NISL
    own = lax.broadcasted_iota(jnp.int32, (rows, rows * NISL), 1) // NISL == (
        lax.broadcasted_iota(jnp.int32, (rows, rows * NISL), 0)
    )
    for b in range(n_dep):
        for copy in copies(b):
            copy.wait()
        for d in range(share):
            at = b * share + d
            z, m, t = (ref[at].astype(jnp.float32) for ref in (dz, dm, dt))
            value = levels(z * east_thick + t * east_base)
            east[b, d * rows : (d + 1) * rows, :] = value
            small[b, d : d + 1, :] = jnp.sum(value, axis=0, keepdims=True)
            north[d * rows : (d + 1) * rows, :] = levels(m * north_thick + t * north_base)
        value = north[...]
        high = value.astype(jnp.bfloat16)
        low = (value - high.astype(jnp.float32)).astype(jnp.bfloat16)
        sums = lax.dot_general(
            jnp.concatenate([high, low], axis=1), hot, (((1,), (1,)), ((), ())),
            preferred_element_type=jnp.float32,
        )
        sums = jnp.where(own[None], sums.reshape(share, rows, rows * NISL), 0.0)
        sums = sums[:, :, :cols] + sums[:, :, cols:]
        sums = jnp.sum(sums, axis=1)
        sums = sums + pltpu.roll(sums, cols // 2, 1)
        sums = sums + pltpu.roll(sums, cols // 4, 1)
        first, second = sums[:8], sums[8:]
        small[b, share:, :] = jnp.where(
            group < 2,
            jnp.where(group == 0, first, pltpu.roll(first, 4, 0)),
            jnp.where(group == 2, second, pltpu.roll(second, 4, 0)),
        )


def depth_kernel(arrived, out):
    value = arrived[0]
    for b in range(1, arrived.shape[0]):
        value = value + arrived[b]
    for p in range(out.shape[0]):
        out[p] = value


def stream_kernel(n_lon, east, arrived, island, out):
    share, rows, cols = out.shape
    mine = lax.axis_index("lat")
    lon = lax.axis_index("lon")
    n_lat = arrived.shape[0] // n_lon
    value = east[0]
    for b in range(1, east.shape[0]):
        value = value + east[b]
    running = value.reshape(share, rows, cols)
    row = lax.broadcasted_iota(jnp.int32, (share, rows, cols), 1)
    step = 1
    while step < rows:
        running = running + jnp.where(row >= step, pltpu.roll(running, step, 1), 0.0)
        step *= 2
    before = jnp.zeros((share, cols), jnp.float32)
    circ = arrived[0, share:, :]
    for p in range(1, arrived.shape[0]):
        circ = circ + arrived[p, share:, :]
    for i in range(n_lat - 1):
        before = before + jnp.where(i < mine, arrived[i * n_lon + lon, :share, :], 0.0)
    label = island[...]
    some = label > 0
    place = jnp.maximum(label - 1, 0)
    for d in range(share):
        g, r = d // 4, d % 4
        constant = jnp.take_along_axis(
            jnp.broadcast_to(circ[r : r + 1, :], (rows, cols)), place + g * NISL, axis=1
        )
        out[d] = running[d] + before[d : d + 1, :] + jnp.where(some, constant, 0.0)


def shards(thick, zonal, merid, d_zonal, d_merid, d_thick, land_sea, line_label, island_label):
    dirs, levels, rows, cols = d_zonal.shape
    n_lat = lax.axis_size("lat")
    n_lon = lax.axis_size("lon")
    n_dep = lax.axis_size("dep")
    share = dirs // n_dep
    level_scale = 1.0 / math.sqrt(levels * n_dep)
    row_scale = 1.0 / math.sqrt(rows * n_lat)
    line_scale = 1.0 / math.sqrt(rows * n_lat * cols * n_lon / (NISL + 1))
    deep = levels * rows
    base = [x.reshape(deep, cols) for x in (thick, zonal, merid, land_sea)]
    moving = [x.reshape(dirs, deep, cols) for x in (d_zonal, d_merid, d_thick)]
    vmem = pl.BlockSpec(memory_space=pltpu.VMEM)
    hbm = pl.BlockSpec(memory_space=pltpu.HBM)
    params = pltpu.CompilerParams(vmem_limit_bytes=VMEM_BYTES)
    east, small = pl.pallas_call(
        functools.partial(transport_kernel, -level_scale * row_scale, level_scale * line_scale),
        out_shape=(
            jax.ShapeDtypeStruct((n_dep, share * rows, cols), jnp.float32),
            jax.ShapeDtypeStruct((n_dep, share + 8, cols), jnp.float32),
        ),
        in_specs=[hbm] * 8,
        out_specs=(vmem, vmem),
        scratch_shapes=[pltpu.VMEM((deep, cols), jnp.float32)] * 3
        + [pltpu.VMEM((deep, cols), jnp.int32), pltpu.VMEM((rows, cols), jnp.int32)]
        + [pltpu.VMEM((dirs, deep, cols), jnp.bfloat16)] * 3
        + [
            pltpu.VMEM((share * rows, cols), jnp.float32),
            pltpu.SemaphoreType.DMA((5,)),
            pltpu.SemaphoreType.DMA((3, n_dep)),
        ],
        compiler_params=params,
        name="transport",
    )(*(pltpu.with_memory_space_constraint(x, pltpu.HBM) for x in (*base, line_label, *moving)))
    east = lax.all_to_all(east, "dep", 0, 0)
    small = lax.all_to_all(small, "dep", 0, 0)
    small = pl.pallas_call(
        depth_kernel,
        out_shape=jax.ShapeDtypeStruct((n_lat * n_lon, share + 8, cols), jnp.float32),
        in_specs=[vmem],
        out_specs=vmem,
        compiler_params=params,
        name="depth",
    )(small)
    small = lax.all_to_all(small, ("lat", "lon"), 0, 0)
    return pl.pallas_call(
        functools.partial(stream_kernel, n_lon),
        out_shape=jax.ShapeDtypeStruct((share, rows, cols), jnp.float32),
        in_specs=[vmem] * 3,
        out_specs=vmem,
        compiler_params=params,
        name="stream",
    )(east, small, island_label)


def solution(mesh):
    return jax.shard_map(
        shards,
        mesh=mesh,
        in_specs=(
            P("dep", "lat", "lon"),
            P("dep", "lat", "lon"),
            P("dep", "lat", "lon"),
            P(None, "dep", "lat", "lon"),
            P(None, "dep", "lat", "lon"),
            P(None, "dep", "lat", "lon"),
            P("dep", "lat", "lon"),
            P("lat", "lon"),
            P("lat", "lon"),
        ),
        out_specs=P("dep", "lat", "lon"),
        check_vma=False,
    )
```

```python
import functools
import math

import jax
import jax.numpy as jnp
from jax import lax
from jax.experimental import pallas as pl
from jax.experimental.pallas import tpu as pltpu
from jax.sharding import PartitionSpec as P

NISL = 32
VMEM_BYTES = 16 * 1024 * 1024


def transport_kernel(
    east_scale, north_scale, thick_hbm, zonal_hbm, merid_hbm, sea_hbm, line_hbm, dz_hbm, dm_hbm,
    dt_hbm, *refs,
):
    (*east, small, thick, zonal, merid, sea, line, dz, dm, dt, north, base_sems, sems) = refs
    n_dep = len(east)
    mine = lax.axis_index("dep")
    share = dz.shape[0] // n_dep
    rows, cols = line.shape
    deep = dz.shape[1]
    base = [
        pltpu.make_async_copy(src, dst, base_sems.at[k])
        for k, (src, dst) in enumerate(
            (
                (thick_hbm, thick), (zonal_hbm, zonal), (merid_hbm, merid), (sea_hbm, sea),
                (line_hbm, line),
            )
        )
    ]

    def copies(b):
        part = pl.ds((mine ^ b) * share, share)
        return [
            pltpu.make_async_copy(src.at[part], dst.at[part], sems.at[k, b])
            for k, (src, dst) in enumerate(((dz_hbm, dz), (dm_hbm, dm), (dt_hbm, dt)))
        ]

    for copy in base:
        copy.start()
    for b in reversed(range(n_dep)):
        for copy in copies(b):
            copy.start()
    for copy in base:
        copy.wait()
    wet = sea[...].astype(jnp.float32)
    east_thick = wet * thick[...] * east_scale
    east_base = wet * zonal[...] * east_scale
    north_thick = wet * thick[...] * north_scale
    north_base = wet * merid[...] * north_scale
    labels = lax.broadcasted_iota(jnp.int32, (NISL, cols), 0) + 1
    hot = jnp.concatenate(
        [(line[i : i + 1, :] == labels).astype(jnp.bfloat16) for i in range(rows)], axis=0
    )
    hot = jnp.concatenate([hot, hot], axis=1)

    def levels(value):
        return jnp.sum(value.reshape(deep // rows, rows, cols), axis=0)

    group = lax.broadcasted_iota(jnp.int32, (rows, cols), 1) // NISL
    own = lax.broadcasted_iota(jnp.int32, (rows, rows * NISL), 1) // NISL == (
        lax.broadcasted_iota(jnp.int32, (rows, rows * NISL), 0)
    )
    for b in reversed(range(n_dep)):
        for copy in copies(b):
            copy.wait()
        for d in range(share):
            at = (mine ^ b) * share + d
            z, m, t = (ref[at].astype(jnp.float32) for ref in (dz, dm, dt))
            value = levels(z * east_thick + t * east_base)
            east[b][d * rows : (d + 1) * rows, :] = value
            small[b, d : d + 1, :] = jnp.sum(value, axis=0, keepdims=True)
            north[d * rows : (d + 1) * rows, :] = levels(m * north_thick + t * north_base)
        value = north[...]
        high = value.astype(jnp.bfloat16)
        low = (value - high.astype(jnp.float32)).astype(jnp.bfloat16)
        sums = lax.dot_general(
            jnp.concatenate([high, low], axis=1), hot, (((1,), (1,)), ((), ())),
            preferred_element_type=jnp.float32,
        )
        sums = jnp.where(own[None], sums.reshape(share, rows, rows * NISL), 0.0)
        sums = sums[:, :, :cols] + sums[:, :, cols:]
        sums = jnp.sum(sums, axis=1)
        sums = sums + pltpu.roll(sums, cols // 2, 1)
        sums = sums + pltpu.roll(sums, cols // 4, 1)
        first, second = sums[:8], sums[8:]
        small[b, share:, :] = jnp.where(
            group < 2,
            jnp.where(group == 0, first, pltpu.roll(first, 4, 0)),
            jnp.where(group == 2, second, pltpu.roll(second, 4, 0)),
        )


def pairs(count, bit):
    return [(i, i ^ bit) for i in range(count)]


def lat_kernel(bit, last, small, arrived, *refs):
    before, out = refs[-2:]
    share = before.shape[1]
    part = jnp.where((lax.axis_index("lat") & bit) != 0, arrived[:, :share, :], 0.0)
    before[...] = part if len(refs) == 2 else refs[0][...] + part
    out[...] = (small[...] + arrived[...])[:, share:, :] if last else small[...] + arrived[...]


def lon_kernel(circ, arrived, before, out):
    share = before.shape[1]
    out[:, :share, :] = before[...]
    out[:, share:, :] = circ[...] + arrived[...]


def stream_kernel(n_dep, *refs):
    east, small, island, out = refs[:n_dep], refs[n_dep : 2 * n_dep], refs[2 * n_dep], refs[-1]
    share, rows, cols = out.shape
    value = sum((ref[...] for ref in east[1:]), east[0][...])
    running = value.reshape(share, rows, cols)
    row = lax.broadcasted_iota(jnp.int32, (share, rows, cols), 1)
    step = 1
    while step < rows:
        running = running + jnp.where(row >= step, pltpu.roll(running, step, 1), 0.0)
        step *= 2
    value = small[0][0]
    for ref in small[1:]:
        value = value + ref[...]
    before, circ = value[:share], value[share:]
    label = island[...]
    some = label > 0
    place = jnp.maximum(label - 1, 0)
    for d in range(share):
        g, r = d // 4, d % 4
        constant = jnp.take_along_axis(
            jnp.broadcast_to(circ[r : r + 1, :], (rows, cols)), place + g * NISL, axis=1
        )
        out[d] = running[d] + before[d : d + 1, :] + jnp.where(some, constant, 0.0)


def shards(thick, zonal, merid, d_zonal, d_merid, d_thick, land_sea, line_label, island_label):
    dirs, levels, rows, cols = d_zonal.shape
    n_lat = lax.axis_size("lat")
    n_lon = lax.axis_size("lon")
    n_dep = lax.axis_size("dep")
    share = dirs // n_dep
    level_scale = 1.0 / math.sqrt(levels * n_dep)
    row_scale = 1.0 / math.sqrt(rows * n_lat)
    line_scale = 1.0 / math.sqrt(rows * n_lat * cols * n_lon / (NISL + 1))
    deep = levels * rows
    base = [x.reshape(deep, cols) for x in (thick, zonal, merid, land_sea)]
    moving = [x.reshape(dirs, deep, cols) for x in (d_zonal, d_merid, d_thick)]
    vmem = pl.BlockSpec(memory_space=pltpu.VMEM)
    hbm = pl.BlockSpec(memory_space=pltpu.HBM)
    params = pltpu.CompilerParams(vmem_limit_bytes=VMEM_BYTES)
    *east, small = pl.pallas_call(
        functools.partial(transport_kernel, -level_scale * row_scale, level_scale * line_scale),
        out_shape=[jax.ShapeDtypeStruct((share * rows, cols), jnp.float32)] * n_dep
        + [jax.ShapeDtypeStruct((n_dep, share + 8, cols), jnp.float32)],
        in_specs=[hbm] * 8,
        out_specs=[vmem] * (n_dep + 1),
        scratch_shapes=[pltpu.VMEM((deep, cols), jnp.float32)] * 3
        + [pltpu.VMEM((deep, cols), jnp.int32), pltpu.VMEM((rows, cols), jnp.int32)]
        + [pltpu.VMEM((dirs, deep, cols), jnp.bfloat16)] * 3
        + [
            pltpu.VMEM((share * rows, cols), jnp.float32),
            pltpu.SemaphoreType.DMA((5,)),
            pltpu.SemaphoreType.DMA((3, n_dep)),
        ],
        compiler_params=params,
        name="transport",
    )(*(pltpu.with_memory_space_constraint(x, pltpu.HBM) for x in (*base, line_label, *moving)))
    for s in range(1, n_dep):
        east[s] = lax.ppermute(east[s], "dep", pairs(n_dep, s))
    before = []
    bit = 1
    while bit < n_lat:
        last = 2 * bit >= n_lat
        arrived = lax.ppermute(small, "lat", pairs(n_lat, bit))
        *before, small = pl.pallas_call(
            functools.partial(lat_kernel, bit, last),
            out_shape=(
                jax.ShapeDtypeStruct((n_dep, share, cols), jnp.float32),
                jax.ShapeDtypeStruct((n_dep, 8 if last else share + 8, cols), jnp.float32),
            ),
            in_specs=[vmem] * (2 + len(before)),
            out_specs=(vmem, vmem),
            compiler_params=params,
            name="bands",
        )(small, arrived, *before)
        bit *= 2
    bit = 1
    while 2 * bit < n_lon:
        small = small + lax.ppermute(small, "lon", pairs(n_lon, bit))
        bit *= 2
    small = pl.pallas_call(
        lon_kernel,
        out_shape=jax.ShapeDtypeStruct((n_dep, share + 8, cols), jnp.float32),
        in_specs=[vmem] * 3,
        out_specs=vmem,
        compiler_params=params,
        name="lines",
    )(small, lax.ppermute(small, "lon", pairs(n_lon, bit)), *before)
    small = [small] + [lax.ppermute(small[s], "dep", pairs(n_dep, s)) for s in range(1, n_dep)]
    return pl.pallas_call(
        functools.partial(stream_kernel, n_dep),
        out_shape=jax.ShapeDtypeStruct((share, rows, cols), jnp.float32),
        in_specs=[vmem] * (2 * n_dep + 1),
        out_specs=vmem,
        compiler_params=params,
        name="stream",
    )(*east, *small, island_label)


def solution(mesh):
    return jax.shard_map(
        shards,
        mesh=mesh,
        in_specs=(
            P("dep", "lat", "lon"),
            P("dep", "lat", "lon"),
            P("dep", "lat", "lon"),
            P(None, "dep", "lat", "lon"),
            P(None, "dep", "lat", "lon"),
            P(None, "dep", "lat", "lon"),
            P("dep", "lat", "lon"),
            P("lat", "lon"),
            P("lat", "lon"),
        ),
        out_specs=P("dep", "lat", "lon"),
        check_vma=False,
    )
```

```python
import functools
import math

import jax
import jax.numpy as jnp
from jax import lax
from jax.experimental import pallas as pl
from jax.experimental.pallas import tpu as pltpu
from jax.sharding import PartitionSpec as P

NISL = 32
VMEM_BYTES = 16 * 1024 * 1024


def transport_kernel(
    east_scale, north_scale, thick_hbm, zonal_hbm, merid_hbm, sea_hbm, line_hbm, dz_hbm, dm_hbm,
    dt_hbm, *refs,
):
    (*east, small, thick, zonal, merid, sea, line, dz, dm, dt, north, base_sems, sems) = refs
    n_dep = len(east)
    mine = lax.axis_index("dep")
    share = dz.shape[0] // n_dep
    rows, cols = line.shape
    deep = dz.shape[1]
    base = [
        pltpu.make_async_copy(src, dst, base_sems.at[k])
        for k, (src, dst) in enumerate(
            (
                (thick_hbm, thick), (zonal_hbm, zonal), (merid_hbm, merid), (sea_hbm, sea),
                (line_hbm, line),
            )
        )
    ]

    def copies(b):
        part = pl.ds((mine ^ b) * share, share)
        return [
            pltpu.make_async_copy(src.at[part], dst.at[part], sems.at[k, b])
            for k, (src, dst) in enumerate(((dz_hbm, dz), (dm_hbm, dm), (dt_hbm, dt)))
        ]

    for copy in base:
        copy.start()
    for b in reversed(range(n_dep)):
        for copy in copies(b):
            copy.start()
    for copy in base:
        copy.wait()
    wet = sea[...].astype(jnp.float32)
    east_thick = wet * thick[...] * east_scale
    east_base = wet * zonal[...] * east_scale
    north_thick = wet * thick[...] * north_scale
    north_base = wet * merid[...] * north_scale

    def levels(value):
        return jnp.sum(value.reshape(deep // rows, rows, cols), axis=0)

    for b in reversed(range(n_dep)):
        for copy in copies(b):
            copy.wait()
        for d in range(share):
            at = (mine ^ b) * share + d
            z, m, t = (ref[at].astype(jnp.float32) for ref in (dz, dm, dt))
            value = levels(z * east_thick + t * east_base)
            east[b][d * rows : (d + 1) * rows, :] = value
            small[b, d : d + 1, :] = jnp.sum(value, axis=0, keepdims=True)
            at = (b * share + d) * rows
            north[at : at + rows, :] = levels(m * north_thick + t * north_base)
    labels = lax.broadcasted_iota(jnp.int32, (NISL, cols), 0) + 1
    hot = jnp.concatenate(
        [(line[i : i + 1, :] == labels).astype(jnp.bfloat16) for i in range(rows)], axis=1
    )
    dirs = n_dep * share
    value = jnp.concatenate([north[pl.ds(i, dirs, stride=rows), :] for i in range(rows)], axis=1)
    high = value.astype(jnp.bfloat16)
    low = (value - high.astype(jnp.float32)).astype(jnp.bfloat16)
    sums = lax.dot_general(
        jnp.concatenate([high, low], axis=0), hot, (((1,), (1,)), ((), ())),
        preferred_element_type=jnp.float32,
    )
    sums = sums[:dirs] + sums[dirs:]
    quarter = share // 4
    lines = [
        jnp.concatenate(
            [sums[b * share + g * quarter : b * share + (g + 1) * quarter] for g in range(4)],
            axis=1,
        )
        for b in range(n_dep)
    ]
    for b in range(n_dep):
        small[b, share : share + quarter, :] = lines[b]
        small[b, share + quarter :, :] = jnp.zeros((8 - quarter, cols), jnp.float32)


def pairs(count, bit):
    return [(i, i ^ bit) for i in range(count)]


def lat_kernel(bit, last, small, arrived, *refs):
    before, out = refs[-2:]
    share = before.shape[1]
    part = jnp.where((lax.axis_index("lat") & bit) != 0, arrived[:, :share, :], 0.0)
    before[...] = part if len(refs) == 2 else refs[0][...] + part
    out[...] = (small[...] + arrived[...])[:, share:, :] if last else small[...] + arrived[...]


def lon_kernel(circ, arrived, before, east, more, near, far, total):
    share = before.shape[1]
    for k in range(2):
        for out, at in ((near, k), (far, 2 + k)):
            out[k, :share, :] = before[at]
            out[k, share:, :] = circ[at] + arrived[at]
    total[...] = east[...] + more[...]


def far_kernel(near, arrived, east, more, own, out, total):
    own[...] = near[0] + arrived[0]
    out[...] = near[1] + arrived[1]
    total[...] = east[...] + more[...]


def stream_kernel(east, more, small, arrived, island, out):
    share, rows, cols = out.shape
    running = (east[...] + more[...]).reshape(share, rows, cols)
    row = lax.broadcasted_iota(jnp.int32, (share, rows, cols), 1)
    step = 1
    while step < rows:
        running = running + jnp.where(row >= step, pltpu.roll(running, step, 1), 0.0)
        step *= 2
    value = small[...] + arrived[...]
    before, circ = value[:share], value[share:]
    label = island[...]
    some = label > 0
    place = jnp.maximum(label - 1, 0)
    for d in range(share):
        g, r = d // 4, d % 4
        constant = jnp.take_along_axis(
            jnp.broadcast_to(circ[r : r + 1, :], (rows, cols)), place + g * NISL, axis=1
        )
        out[d] = running[d] + before[d : d + 1, :] + jnp.where(some, constant, 0.0)


def shards(thick, zonal, merid, d_zonal, d_merid, d_thick, land_sea, line_label, island_label):
    dirs, levels, rows, cols = d_zonal.shape
    n_lat = lax.axis_size("lat")
    n_lon = lax.axis_size("lon")
    n_dep = lax.axis_size("dep")
    share = dirs // n_dep
    level_scale = 1.0 / math.sqrt(levels * n_dep)
    row_scale = 1.0 / math.sqrt(rows * n_lat)
    line_scale = 1.0 / math.sqrt(rows * n_lat * cols * n_lon / (NISL + 1))
    deep = levels * rows
    base = [x.reshape(deep, cols) for x in (thick, zonal, merid, land_sea)]
    moving = [x.reshape(dirs, deep, cols) for x in (d_zonal, d_merid, d_thick)]
    vmem = pl.BlockSpec(memory_space=pltpu.VMEM)
    hbm = pl.BlockSpec(memory_space=pltpu.HBM)
    params = pltpu.CompilerParams(vmem_limit_bytes=VMEM_BYTES)
    *east, small = pl.pallas_call(
        functools.partial(transport_kernel, -level_scale * row_scale, level_scale * line_scale),
        out_shape=[jax.ShapeDtypeStruct((share * rows, cols), jnp.float32)] * n_dep
        + [jax.ShapeDtypeStruct((n_dep, share + 8, cols), jnp.float32)],
        in_specs=[hbm] * 8,
        out_specs=[vmem] * (n_dep + 1),
        scratch_shapes=[pltpu.VMEM((deep, cols), jnp.float32)] * 3
        + [pltpu.VMEM((deep, cols), jnp.int32), pltpu.VMEM((rows, cols), jnp.int32)]
        + [pltpu.VMEM((dirs, deep, cols), jnp.bfloat16)] * 3
        + [
            pltpu.VMEM((dirs * rows, cols), jnp.float32),
            pltpu.SemaphoreType.DMA((5,)),
            pltpu.SemaphoreType.DMA((3, n_dep)),
        ],
        compiler_params=params,
        name="transport",
    )(*(pltpu.with_memory_space_constraint(x, pltpu.HBM) for x in (*base, line_label, *moving)))
    east[3] = lax.ppermute(east[3], "dep", pairs(n_dep, 3))
    before = []
    bit = 1
    while bit < n_lat:
        last = 2 * bit >= n_lat
        arrived = lax.ppermute(small, "lat", pairs(n_lat, bit))
        *before, small = pl.pallas_call(
            functools.partial(lat_kernel, bit, last),
            out_shape=(
                jax.ShapeDtypeStruct((n_dep, share, cols), jnp.float32),
                jax.ShapeDtypeStruct((n_dep, 8 if last else share + 8, cols), jnp.float32),
            ),
            in_specs=[vmem] * (2 + len(before)),
            out_specs=(vmem, vmem),
            compiler_params=params,
            name="bands",
        )(small, arrived, *before)
        bit *= 2
    small, east[2] = lax.optimization_barrier((small, east[2]))
    east[2] = lax.ppermute(east[2], "dep", pairs(n_dep, 2))
    bit = 1
    while 2 * bit < n_lon:
        small = small + lax.ppermute(small, "lon", pairs(n_lon, bit))
        bit *= 2
    block = jax.ShapeDtypeStruct((share + 8, cols), jnp.float32)
    two = jax.ShapeDtypeStruct((2, share + 8, cols), jnp.float32)
    full = jax.ShapeDtypeStruct((share * rows, cols), jnp.float32)
    near, far, total = pl.pallas_call(
        lon_kernel,
        out_shape=(two, two, full),
        in_specs=[vmem] * 5,
        out_specs=[vmem] * 3,
        compiler_params=params,
        name="lines",
    )(small, lax.ppermute(small, "lon", pairs(n_lon, bit)), *before, east[0], east[3])
    far, east[1] = lax.optimization_barrier((far, east[1]))
    east[1] = lax.ppermute(east[1], "dep", pairs(n_dep, 1))
    own, out, total = pl.pallas_call(
        far_kernel,
        out_shape=(block, block, full),
        in_specs=[vmem] * 4,
        out_specs=[vmem] * 3,
        compiler_params=params,
        name="depths",
    )(near, lax.ppermute(far, "dep", pairs(n_dep, 2)), total, east[2])
    return pl.pallas_call(
        stream_kernel,
        out_shape=jax.ShapeDtypeStruct((share, rows, cols), jnp.float32),
        in_specs=[vmem] * 5,
        out_specs=vmem,
        compiler_params=params,
        name="stream",
    )(total, east[1], own, lax.ppermute(out, "dep", pairs(n_dep, 1)), island_label)


def solution(mesh):
    return jax.shard_map(
        shards,
        mesh=mesh,
        in_specs=(
            P("dep", "lat", "lon"),
            P("dep", "lat", "lon"),
            P("dep", "lat", "lon"),
            P(None, "dep", "lat", "lon"),
            P(None, "dep", "lat", "lon"),
            P(None, "dep", "lat", "lon"),
            P("dep", "lat", "lon"),
            P("lat", "lon"),
            P("lat", "lon"),
        ),
        out_specs=P("dep", "lat", "lon"),
        check_vma=False,
    )
```

```python
import functools
import math

import jax
import jax.numpy as jnp
from jax import lax
from jax.experimental import pallas as pl
from jax.experimental.pallas import tpu as pltpu
from jax.sharding import PartitionSpec as P

NISL = 32
VMEM_BYTES = 16 * 1024 * 1024
LARGE = 600_000_000


def transport_kernel(
    east_scale, north_scale, thick_hbm, zonal_hbm, merid_hbm, sea_hbm, line_hbm, dz_hbm, dm_hbm,
    dt_hbm, *refs,
):
    (*east, near, far, thick, zonal, merid, sea, line, dz, dm, dt, north, base_sems, sems) = refs
    n_dep = len(east)
    small = [near.at[0], near.at[1], far.at[0], far.at[1]]
    mine = lax.axis_index("dep")
    share = dz.shape[0] // n_dep
    rows, cols = line.shape
    deep = dz.shape[1]
    base = [
        pltpu.make_async_copy(src, dst, base_sems.at[k])
        for k, (src, dst) in enumerate(
            (
                (thick_hbm, thick), (zonal_hbm, zonal), (merid_hbm, merid), (sea_hbm, sea),
                (line_hbm, line),
            )
        )
    ]

    def copies(b):
        part = pl.ds((mine ^ b) * share, share)
        return [
            pltpu.make_async_copy(src.at[part], dst.at[part], sems.at[k, b])
            for k, (src, dst) in enumerate(((dz_hbm, dz), (dm_hbm, dm), (dt_hbm, dt)))
        ]

    for copy in base:
        copy.start()
    for b in reversed(range(n_dep)):
        for copy in copies(b):
            copy.start()
    for copy in base:
        copy.wait()
    wet = sea[...].astype(jnp.float32)
    east_thick = wet * thick[...] * east_scale
    east_base = wet * zonal[...] * east_scale
    north_thick = wet * thick[...] * north_scale
    north_base = wet * merid[...] * north_scale

    def levels(value):
        return jnp.sum(value.reshape(deep // rows, rows, cols), axis=0)

    for b in reversed(range(n_dep)):
        for copy in copies(b):
            copy.wait()
        for d in range(share):
            at = (mine ^ b) * share + d
            z, m, t = (ref[at].astype(jnp.float32) for ref in (dz, dm, dt))
            value = levels(z * east_thick + t * east_base)
            east[b][d * rows : (d + 1) * rows, :] = value
            small[b][d : d + 1, :] = jnp.sum(value, axis=0, keepdims=True)
            at = (b * share + d) * rows
            north[at : at + rows, :] = levels(m * north_thick + t * north_base)
    labels = lax.broadcasted_iota(jnp.int32, (NISL, cols), 0) + 1
    hot = jnp.concatenate(
        [(line[i : i + 1, :] == labels).astype(jnp.bfloat16) for i in range(rows)], axis=1
    )
    dirs = n_dep * share
    value = jnp.concatenate([north[pl.ds(i, dirs, stride=rows), :] for i in range(rows)], axis=1)
    high = value.astype(jnp.bfloat16)
    low = (value - high.astype(jnp.float32)).astype(jnp.bfloat16)
    sums = lax.dot_general(
        jnp.concatenate([high, low], axis=0), hot, (((1,), (1,)), ((), ())),
        preferred_element_type=jnp.float32,
    )
    sums = sums[:dirs] + sums[dirs:]
    quarter = share // 4
    lines = [
        jnp.concatenate(
            [sums[b * share + g * quarter : b * share + (g + 1) * quarter] for g in range(4)],
            axis=1,
        )
        for b in range(n_dep)
    ]
    for b in range(n_dep):
        small[b][share : share + quarter, :] = lines[b]
        small[b][share + quarter :, :] = jnp.zeros((8 - quarter, cols), jnp.float32)


def stage(part):
    return pl.CostEstimate(flops=int(part * LARGE), bytes_accessed=0, transcendentals=0)


def pairs(count, bit):
    return [(i, i ^ bit) for i in range(count)]


def far_kernel(near, arrived, own, out):
    own[...] = near[0] + arrived[0]
    out[...] = near[1] + arrived[1]


def near_kernel(own, arrived, out):
    out[...] = own[...] + arrived[...]


def lat_kernel(bit, last, small, arrived, *refs):
    if last:
        *refs, east, more, total, before, out = refs
        total[...] = east[...] + more[...]
        refs = (*refs, before, out)
    before, out = refs[-2:]
    share = before.shape[0]
    part = jnp.where((lax.axis_index("lat") & bit) != 0, arrived[:share, :], 0.0)
    before[...] = part if len(refs) == 2 else refs[0][...] + part
    out[...] = (small[...] + arrived[...])[share:, :] if last else small[...] + arrived[...]


def lon_kernel(circ, arrived, east, more, out, total):
    out[...] = circ[...] + arrived[...]
    total[...] = east[...] + more[...]


def stream_kernel(east, more, before, lines, island, out):
    share, rows, cols = out.shape
    running = (east[...] + more[...]).reshape(share, rows, cols)
    row = lax.broadcasted_iota(jnp.int32, (share, rows, cols), 1)
    step = 1
    while step < rows:
        running = running + jnp.where(row >= step, pltpu.roll(running, step, 1), 0.0)
        step *= 2
    circ = lines[...]
    label = island[...]
    some = label > 0
    place = jnp.maximum(label - 1, 0)
    for d in range(share):
        g, r = d // 4, d % 4
        constant = jnp.take_along_axis(
            jnp.broadcast_to(circ[r : r + 1, :], (rows, cols)), place + g * NISL, axis=1
        )
        out[d] = running[d] + before[d : d + 1, :] + jnp.where(some, constant, 0.0)


def shards(thick, zonal, merid, d_zonal, d_merid, d_thick, land_sea, line_label, island_label):
    dirs, levels, rows, cols = d_zonal.shape
    n_lat = lax.axis_size("lat")
    n_lon = lax.axis_size("lon")
    n_dep = lax.axis_size("dep")
    share = dirs // n_dep
    level_scale = 1.0 / math.sqrt(levels * n_dep)
    row_scale = 1.0 / math.sqrt(rows * n_lat)
    line_scale = 1.0 / math.sqrt(rows * n_lat * cols * n_lon / (NISL + 1))
    deep = levels * rows
    base = [x.reshape(deep, cols) for x in (thick, zonal, merid, land_sea)]
    moving = [x.reshape(dirs, deep, cols) for x in (d_zonal, d_merid, d_thick)]
    vmem = pl.BlockSpec(memory_space=pltpu.VMEM)
    hbm = pl.BlockSpec(memory_space=pltpu.HBM)
    params = pltpu.CompilerParams(vmem_limit_bytes=VMEM_BYTES)
    block = jax.ShapeDtypeStruct((share + 8, cols), jnp.float32)
    two = jax.ShapeDtypeStruct((2, share + 8, cols), jnp.float32)
    full = jax.ShapeDtypeStruct((share * rows, cols), jnp.float32)
    *east, near, far = pl.pallas_call(
        functools.partial(transport_kernel, -level_scale * row_scale, level_scale * line_scale),
        out_shape=[full] * n_dep
        + [two, two],
        in_specs=[hbm] * 8,
        out_specs=[vmem] * (n_dep + 2),
        scratch_shapes=[pltpu.VMEM((deep, cols), jnp.float32)] * 3
        + [pltpu.VMEM((deep, cols), jnp.int32), pltpu.VMEM((rows, cols), jnp.int32)]
        + [pltpu.VMEM((dirs, deep, cols), jnp.bfloat16)] * 3
        + [
            pltpu.VMEM((dirs * rows, cols), jnp.float32),
            pltpu.SemaphoreType.DMA((5,)),
            pltpu.SemaphoreType.DMA((3, n_dep)),
        ],
        compiler_params=params,
        name="transport",
    )(*(pltpu.with_memory_space_constraint(x, pltpu.HBM) for x in (*base, line_label, *moving)))
    own, out = pl.pallas_call(
        far_kernel,
        out_shape=(block, block),
        in_specs=[vmem] * 2,
        out_specs=[vmem] * 2,
        compiler_params=params,
        name="far",
    )(near, lax.ppermute(far, "dep", pairs(n_dep, 2)))
    out, east[3] = lax.optimization_barrier((out, east[3]))
    east[3] = lax.ppermute(east[3], "dep", pairs(n_dep, 3))
    small = pl.pallas_call(
        near_kernel,
        out_shape=block,
        in_specs=[vmem] * 2,
        out_specs=vmem,
        compiler_params=params,
        cost_estimate=stage(0.7),
        name="near",
    )(own, lax.ppermute(out, "dep", pairs(n_dep, 1)))
    small, east[2] = lax.optimization_barrier((small, east[2]))
    east[2] = lax.ppermute(east[2], "dep", pairs(n_dep, 2))
    before = []
    bit = 1
    while bit < n_lat:
        last = 2 * bit >= n_lat
        arrived = lax.ppermute(small, "lat", pairs(n_lat, bit))
        extra = (east[0], east[3]) if last else ()
        *before, small = pl.pallas_call(
            functools.partial(lat_kernel, bit, last),
            out_shape=[full] * last
            + [
                jax.ShapeDtypeStruct((share, cols), jnp.float32),
                jax.ShapeDtypeStruct((8 if last else share + 8, cols), jnp.float32),
            ],
            in_specs=[vmem] * (2 + len(before) + len(extra)),
            out_specs=[vmem] * (2 + last),
            compiler_params=params,
            cost_estimate=stage(0.4 if last else 0.7),
            name="bands",
        )(small, arrived, *before, *extra)
        if last:
            total, *before = before
        if bit == 1:
            small, east[1] = lax.optimization_barrier((small, east[1]))
            east[1] = lax.ppermute(east[1], "dep", pairs(n_dep, 1))
        bit *= 2
    bit = 1
    while 2 * bit < n_lon:
        small = small + lax.ppermute(small, "lon", pairs(n_lon, bit))
        bit *= 2
    lines, total = pl.pallas_call(
        lon_kernel,
        out_shape=(jax.ShapeDtypeStruct((8, cols), jnp.float32), full),
        in_specs=[vmem] * 4,
        out_specs=[vmem] * 2,
        compiler_params=params,
        cost_estimate=stage(0.7),
        name="lines",
    )(small, lax.ppermute(small, "lon", pairs(n_lon, bit)), total, east[2])
    return pl.pallas_call(
        stream_kernel,
        out_shape=jax.ShapeDtypeStruct((share, rows, cols), jnp.float32),
        in_specs=[vmem] * 5,
        out_specs=vmem,
        compiler_params=params,
        name="stream",
    )(total, east[1], *before, lines, island_label)


def solution(mesh):
    return jax.shard_map(
        shards,
        mesh=mesh,
        in_specs=(
            P("dep", "lat", "lon"),
            P("dep", "lat", "lon"),
            P("dep", "lat", "lon"),
            P(None, "dep", "lat", "lon"),
            P(None, "dep", "lat", "lon"),
            P(None, "dep", "lat", "lon"),
            P("dep", "lat", "lon"),
            P("lat", "lon"),
            P("lat", "lon"),
        ),
        out_specs=P("dep", "lat", "lon"),
        check_vma=False,
    )
```

```python
import functools
import math

import jax
import jax.numpy as jnp
from jax import lax
from jax.experimental import pallas as pl
from jax.experimental.pallas import tpu as pltpu
from jax.sharding import PartitionSpec as P

NISL = 32
VMEM_BYTES = 16 * 1024 * 1024


def transport_kernel(
    east_scale, north_scale, thick_hbm, zonal_hbm, merid_hbm, sea_hbm, line_hbm, island_hbm, dz_hbm,
    dm_hbm, dt_hbm, own, rest, small, island, thick, zonal, merid, sea, line, dz, dm, dt, north,
    base_sems, sems,
):
    n_dep = small.shape[0]
    east = [own] + [rest.at[s] for s in range(n_dep - 1)]
    mine = lax.axis_index("dep")
    share = dz.shape[0] // n_dep
    rows, cols = line.shape
    deep = dz.shape[1]
    base = [
        pltpu.make_async_copy(src, dst, base_sems.at[k])
        for k, (src, dst) in enumerate(
            (
                (thick_hbm, thick), (zonal_hbm, zonal), (merid_hbm, merid), (sea_hbm, sea),
                (line_hbm, line), (island_hbm, island),
            )
        )
    ]

    def copies(b):
        part = pl.ds((mine ^ b) * share, share)
        return [
            pltpu.make_async_copy(src.at[part], dst.at[part], sems.at[k, b])
            for k, (src, dst) in enumerate(((dz_hbm, dz), (dm_hbm, dm), (dt_hbm, dt)))
        ]

    for copy in base:
        copy.start()
    for b in reversed(range(n_dep)):
        for copy in copies(b):
            copy.start()
    for copy in base:
        copy.wait()
    wet = sea[...].astype(jnp.float32)
    east_thick = wet * thick[...] * east_scale
    east_base = wet * zonal[...] * east_scale
    north_thick = wet * thick[...] * north_scale
    north_base = wet * merid[...] * north_scale

    def levels(value):
        return jnp.sum(value.reshape(deep // rows, rows, cols), axis=0)

    for b in reversed(range(n_dep)):
        for copy in copies(b):
            copy.wait()
        for d in range(share):
            at = (mine ^ b) * share + d
            z, m, t = (ref[at].astype(jnp.float32) for ref in (dz, dm, dt))
            value = levels(z * east_thick + t * east_base)
            east[b][d * rows : (d + 1) * rows, :] = value
            small[b, d : d + 1, :] = jnp.sum(value, axis=0, keepdims=True)
            at = (b * share + d) * rows
            north[at : at + rows, :] = levels(m * north_thick + t * north_base)
    labels = lax.broadcasted_iota(jnp.int32, (NISL, cols), 0) + 1
    hot = jnp.concatenate(
        [(line[i : i + 1, :] == labels).astype(jnp.bfloat16) for i in range(rows)], axis=1
    )
    dirs = n_dep * share
    value = jnp.concatenate([north[pl.ds(i, dirs, stride=rows), :] for i in range(rows)], axis=1)
    high = value.astype(jnp.bfloat16)
    low = (value - high.astype(jnp.float32)).astype(jnp.bfloat16)
    sums = lax.dot_general(
        jnp.concatenate([high, low], axis=0), hot, (((1,), (1,)), ((), ())),
        preferred_element_type=jnp.float32,
    )
    sums = sums[:dirs] + sums[dirs:]
    quarter = share // 4
    lines = [
        jnp.concatenate(
            [sums[b * share + g * quarter : b * share + (g + 1) * quarter] for g in range(4)],
            axis=1,
        )
        for b in range(n_dep)
    ]
    for b in range(n_dep):
        small[b, share : share + quarter, :] = lines[b]
        small[b, share + quarter :, :] = jnp.zeros((8 - quarter, cols), jnp.float32)


def core_kernel(small, arrived, near, far):
    share = small.shape[1] - 8
    for k in range(2):
        for out, at in ((near, k), (far, 2 + k)):
            out[k, :share, :] = arrived[at, :share, :]
            out[k, share:, :] = small[at] + arrived[at]


def far_kernel(near, arrived, own, out):
    own[...] = near[0] + arrived[0]
    out[...] = near[1] + arrived[1]


def near_kernel(own, arrived, first, out):
    value = own[...] + arrived[...]
    share = first.shape[0]
    first[...] = value[:share]
    out[...] = value[share:]


def lat_kernel(bit, small, arrived, *refs):
    before, out = refs[-2:]
    share = before.shape[0]
    part = jnp.where((lax.axis_index("lat") & bit) != 0, arrived[:share, :], 0.0)
    before[...] = part if len(refs) == 2 else refs[0][...] + part
    out[...] = small[...] + arrived[...]


def lon_kernel(small, arrived, before, out):
    share = before.shape[0]
    out[:share, :] = before[...]
    out[share:, :] = small[share:, :] + arrived[share:, :]


def merge_kernel(rest, arrived, *out):
    for s, ref in enumerate(out):
        ref[0] = rest[s]
        ref[1] = arrived[s]


def depth_kernel(*refs):
    *arrived, first, second = refs
    for k, out in enumerate((first, second)):
        value = arrived[0][k]
        for ref in arrived[1:]:
            value = value + ref[k]
        out[...] = value


def stream_kernel(own, first, second, small, small_first, total, island, out):
    share, rows, cols = out.shape
    odd = (lax.axis_index("lat") & 1) != 0
    running = own[...] + jnp.where(odd, second[...], first[...])
    running = running.reshape(share, rows, cols)
    row = lax.broadcasted_iota(jnp.int32, (share, rows, cols), 1)
    step = 1
    while step < rows:
        running = running + jnp.where(row >= step, pltpu.roll(running, step, 1), 0.0)
        step *= 2
    value = jnp.where(odd, small[...], small_first[...])
    before = value[:share] + jnp.where(odd, total[...], 0.0)
    circ = value[share:]
    label = island[...]
    some = label > 0
    place = jnp.maximum(label - 1, 0)
    for d in range(share):
        g, r = d // 4, d % 4
        constant = jnp.take_along_axis(
            jnp.broadcast_to(circ[r : r + 1, :], (rows, cols)), place + g * NISL, axis=1
        )
        out[d] = running[d] + before[d : d + 1, :] + jnp.where(some, constant, 0.0)


def exchange(value, axis, core, bit):
    n_lat = lax.axis_size("lat")
    lats = range(core, n_lat, 2)
    if axis == "lat":
        return lax.ppermute(value, "lat", [(i, i ^ bit) for i in lats])
    count = lax.axis_size(axis)
    return lax.ppermute(
        value, ("lat", axis), [(i * count + j, i * count + (j ^ bit)) for i in lats for j in range(count)]
    )


def shards(thick, zonal, merid, d_zonal, d_merid, d_thick, land_sea, line_label, island_label):
    dirs, levels, rows, cols = d_zonal.shape
    n_lat = lax.axis_size("lat")
    n_lon = lax.axis_size("lon")
    n_dep = lax.axis_size("dep")
    share = dirs // n_dep
    level_scale = 1.0 / math.sqrt(levels * n_dep)
    row_scale = 1.0 / math.sqrt(rows * n_lat)
    line_scale = 1.0 / math.sqrt(rows * n_lat * cols * n_lon / (NISL + 1))
    deep = levels * rows
    base = [x.reshape(deep, cols) for x in (thick, zonal, merid, land_sea)]
    moving = [x.reshape(dirs, deep, cols) for x in (d_zonal, d_merid, d_thick)]
    vmem = pl.BlockSpec(memory_space=pltpu.VMEM)
    hbm = pl.BlockSpec(memory_space=pltpu.HBM)
    params = pltpu.CompilerParams(vmem_limit_bytes=VMEM_BYTES)

    def call(kernel, name, out_shape, *operands):
        return pl.pallas_call(
            kernel,
            out_shape=out_shape,
            in_specs=[vmem] * len(operands),
            out_specs=jax.tree.map(lambda _: vmem, out_shape),
            compiler_params=params,
            name=name,
        )(*operands)

    def shape(*sizes):
        return jax.ShapeDtypeStruct(sizes, jnp.float32)

    full = shape(share * rows, cols)
    own, rest, small, island = pl.pallas_call(
        functools.partial(transport_kernel, -level_scale * row_scale, level_scale * line_scale),
        out_shape=(
            full,
            shape(n_dep - 1, share * rows, cols),
            shape(n_dep, share + 8, cols),
            jax.ShapeDtypeStruct((rows, cols), jnp.int32),
        ),
        in_specs=[hbm] * 9,
        out_specs=[vmem] * 4,
        scratch_shapes=[pltpu.VMEM((deep, cols), jnp.float32)] * 3
        + [pltpu.VMEM((deep, cols), jnp.int32), pltpu.VMEM((rows, cols), jnp.int32)]
        + [pltpu.VMEM((dirs, deep, cols), jnp.bfloat16)] * 3
        + [
            pltpu.VMEM((dirs * rows, cols), jnp.float32),
            pltpu.SemaphoreType.DMA((6,)),
            pltpu.SemaphoreType.DMA((3, n_dep)),
        ],
        compiler_params=params,
        name="transport",
    )(
        *(
            pltpu.with_memory_space_constraint(x, pltpu.HBM)
            for x in (*base, line_label, island_label, *moving)
        )
    )
    arrived = exchange(small, "lat", 0, 1)
    arrived, leaving = lax.optimization_barrier((arrived, rest))
    handed = exchange(leaving, "lat", 1, 1)
    two = shape(2, 2 * share + 8, cols)
    near, far = call(core_kernel, "core", (two, two), small, arrived)
    blocks = call(
        merge_kernel, "merge", [shape(2, share * rows, cols)] * (n_dep - 1), rest, handed
    )
    blocks = [exchange(block, "dep", 0, s + 1) for s, block in enumerate(blocks)]
    first, second = call(depth_kernel, "depth", (full, full), *blocks)
    second = exchange(second, "lat", 0, 1)
    half = shape(2 * share + 8, cols)
    kept, out = call(far_kernel, "far", (half, half), near, exchange(far, "dep", 1, 2))
    total, small = call(
        near_kernel, "near", (shape(share, cols), shape(share + 8, cols)), kept,
        exchange(out, "dep", 1, 1),
    )
    before = []
    bit = 2
    while bit < n_lat:
        *before, small = call(
            functools.partial(lat_kernel, bit), "bands",
            (shape(share, cols), shape(share + 8, cols)),
            small, exchange(small, "lat", 1, bit), *before,
        )
        bit *= 2
    bit = 1
    while 2 * bit < n_lon:
        small = small + exchange(small, "lon", 1, bit)
        bit *= 2
    small = call(
        lon_kernel, "lines", shape(share + 8, cols), small, exchange(small, "lon", 1, bit), *before
    )
    return call(
        stream_kernel, "stream", shape(share, rows, cols),
        own, first, second, small, exchange(small, "lat", 1, 1), total, island,
    )


def solution(mesh):
    return jax.shard_map(
        shards,
        mesh=mesh,
        in_specs=(
            P("dep", "lat", "lon"),
            P("dep", "lat", "lon"),
            P("dep", "lat", "lon"),
            P(None, "dep", "lat", "lon"),
            P(None, "dep", "lat", "lon"),
            P(None, "dep", "lat", "lon"),
            P("dep", "lat", "lon"),
            P("lat", "lon"),
            P("lat", "lon"),
        ),
        out_specs=P("dep", "lat", "lon"),
        check_vma=False,
    )
```

```python
import functools
import math

import jax
import jax.numpy as jnp
from jax import lax
from jax.experimental import pallas as pl
from jax.experimental.pallas import tpu as pltpu
from jax.sharding import PartitionSpec as P

NISL = 32
VMEM_BYTES = 16 * 1024 * 1024


def transport_kernel(
    east_scale, north_scale, thick_hbm, zonal_hbm, merid_hbm, sea_hbm, line_hbm, island_hbm, dz_hbm,
    dm_hbm, dt_hbm, own, rest, small, island, thick, zonal, merid, sea, line, dz, dm, dt, north,
    base_sems, sems,
):
    n_dep = small.shape[0]
    east = [own] + [rest.at[s] for s in range(n_dep - 1)]
    mine = lax.axis_index("dep")
    share = dz.shape[0] // n_dep
    rows, cols = line.shape
    deep = dz.shape[1]
    base = [
        pltpu.make_async_copy(src, dst, base_sems.at[k])
        for k, (src, dst) in enumerate(
            (
                (thick_hbm, thick), (zonal_hbm, zonal), (merid_hbm, merid), (sea_hbm, sea),
                (line_hbm, line), (island_hbm, island),
            )
        )
    ]

    def copies(b):
        part = pl.ds((mine ^ b) * share, share)
        return [
            pltpu.make_async_copy(src.at[part], dst.at[part], sems.at[k, b])
            for k, (src, dst) in enumerate(((dz_hbm, dz), (dm_hbm, dm), (dt_hbm, dt)))
        ]

    for copy in base:
        copy.start()
    for b in reversed(range(n_dep)):
        for copy in copies(b):
            copy.start()
    for copy in base:
        copy.wait()
    wet = sea[...].astype(jnp.float32)
    east_thick = wet * thick[...] * east_scale
    east_base = wet * zonal[...] * east_scale
    north_thick = wet * thick[...] * north_scale
    north_base = wet * merid[...] * north_scale

    def levels(value):
        return jnp.sum(value.reshape(deep // rows, rows, cols), axis=0)

    for b in reversed(range(n_dep)):
        for copy in copies(b):
            copy.wait()
        for d in range(share):
            at = (mine ^ b) * share + d
            z, m, t = (ref[at].astype(jnp.float32) for ref in (dz, dm, dt))
            value = levels(z * east_thick + t * east_base)
            east[b][d * rows : (d + 1) * rows, :] = value
            small[b, d : d + 1, :] = jnp.sum(value, axis=0, keepdims=True)
            at = (b * share + d) * rows
            north[at : at + rows, :] = levels(m * north_thick + t * north_base)
    labels = lax.broadcasted_iota(jnp.int32, (NISL, cols), 0) + 1
    hot = jnp.concatenate(
        [(line[i : i + 1, :] == labels).astype(jnp.bfloat16) for i in range(rows)], axis=1
    )
    dirs = n_dep * share
    value = jnp.concatenate([north[pl.ds(i, dirs, stride=rows), :] for i in range(rows)], axis=1)
    high = value.astype(jnp.bfloat16)
    low = (value - high.astype(jnp.float32)).astype(jnp.bfloat16)
    sums = lax.dot_general(
        jnp.concatenate([high, low], axis=0), hot, (((1,), (1,)), ((), ())),
        preferred_element_type=jnp.float32,
    )
    sums = sums[:dirs] + sums[dirs:]
    quarter = share // 4
    lines = [
        jnp.concatenate(
            [sums[b * share + g * quarter : b * share + (g + 1) * quarter] for g in range(4)],
            axis=1,
        )
        for b in range(n_dep)
    ]
    for b in range(n_dep):
        small[b, share : share + quarter, :] = lines[b]
        small[b, share + quarter :, :] = jnp.zeros((8 - quarter, cols), jnp.float32)


def core_kernel(small, arrived, near, far):
    share = small.shape[1] - 8
    for k in range(2):
        for out, at in ((near, k), (far, 2 + k)):
            out[k, :share, :] = arrived[at, :share, :]
            out[k, share:, :] = small[at] + arrived[at]


def far_kernel(near, arrived, own, out):
    own[...] = near[0] + arrived[0]
    out[...] = near[1] + arrived[1]


def near_kernel(own, arrived, first, out):
    value = own[...] + arrived[...]
    share = first.shape[0]
    first[...] = value[:share]
    out[...] = value[share:]


def lat_kernel(bit, small, arrived, *refs):
    before, out = refs[-2:]
    share = before.shape[0]
    part = jnp.where((lax.axis_index("lat") & bit) != 0, arrived[:share, :], 0.0)
    before[...] = part if len(refs) == 2 else refs[0][...] + part
    out[...] = small[...] + arrived[...]


def lon_kernel(small, arrived, before, out):
    share = before.shape[0]
    out[:share, :] = before[...]
    out[share:, :] = small[share:, :] + arrived[share:, :]


def merge_kernel(rest, arrived, *out):
    for s, ref in enumerate(out):
        ref[0] = rest[s]
        ref[1] = arrived[s]


def depth_kernel(*refs):
    *arrived, first, second = refs
    for k, out in enumerate((first, second)):
        value = arrived[0][k]
        for ref in arrived[1:]:
            value = value + ref[k]
        out[...] = value


def stream_kernel(own, first, second, small, small_first, total, island, out):
    share, rows, cols = out.shape
    odd = (lax.axis_index("lat") & 1) != 0
    running = own[...] + jnp.where(odd, second[...], first[...])
    running = running.reshape(share, rows, cols)
    row = lax.broadcasted_iota(jnp.int32, (share, rows, cols), 1)
    step = 1
    while step < rows:
        running = running + jnp.where(row >= step, pltpu.roll(running, step, 1), 0.0)
        step *= 2
    value = jnp.where(odd, small[...], small_first[...])
    before = value[:share] + jnp.where(odd, total[...], 0.0)
    circ = value[share:]
    label = island[...]
    some = label > 0
    place = jnp.maximum(label - 1, 0)
    for d in range(share):
        g, r = d // 4, d % 4
        constant = jnp.take_along_axis(
            jnp.broadcast_to(circ[r : r + 1, :], (rows, cols)), place + g * NISL, axis=1
        )
        out[d] = running[d] + before[d : d + 1, :] + jnp.where(some, constant, 0.0)


def exchange(value, axis, core, bit):
    n_lat = lax.axis_size("lat")
    count = lax.axis_size(axis)

    def place(i, j):
        other = j ^ bit if core is None or i % 2 == core else j
        return (i * count + j, i * count + other)

    if axis == "lat":
        return lax.ppermute(
            value, "lat", [(i, i ^ bit if core is None or i % 2 == core else i) for i in range(n_lat)]
        )
    return lax.ppermute(
        value, ("lat", axis), [place(i, j) for i in range(n_lat) for j in range(count)]
    )


def shards(thick, zonal, merid, d_zonal, d_merid, d_thick, land_sea, line_label, island_label):
    dirs, levels, rows, cols = d_zonal.shape
    n_lat = lax.axis_size("lat")
    n_lon = lax.axis_size("lon")
    n_dep = lax.axis_size("dep")
    share = dirs // n_dep
    level_scale = 1.0 / math.sqrt(levels * n_dep)
    row_scale = 1.0 / math.sqrt(rows * n_lat)
    line_scale = 1.0 / math.sqrt(rows * n_lat * cols * n_lon / (NISL + 1))
    deep = levels * rows
    base = [x.reshape(deep, cols) for x in (thick, zonal, merid, land_sea)]
    moving = [x.reshape(dirs, deep, cols) for x in (d_zonal, d_merid, d_thick)]
    vmem = pl.BlockSpec(memory_space=pltpu.VMEM)
    hbm = pl.BlockSpec(memory_space=pltpu.HBM)
    params = pltpu.CompilerParams(vmem_limit_bytes=VMEM_BYTES)

    def call(kernel, name, out_shape, *operands):
        return pl.pallas_call(
            kernel,
            out_shape=out_shape,
            in_specs=[vmem] * len(operands),
            out_specs=jax.tree.map(lambda _: vmem, out_shape),
            compiler_params=params,
            name=name,
        )(*operands)

    def shape(*sizes):
        return jax.ShapeDtypeStruct(sizes, jnp.float32)

    full = shape(share * rows, cols)
    own, rest, small, island = pl.pallas_call(
        functools.partial(transport_kernel, -level_scale * row_scale, level_scale * line_scale),
        out_shape=(
            full,
            shape(n_dep - 1, share * rows, cols),
            shape(n_dep, share + 8, cols),
            jax.ShapeDtypeStruct((rows, cols), jnp.int32),
        ),
        in_specs=[hbm] * 9,
        out_specs=[vmem] * 4,
        scratch_shapes=[pltpu.VMEM((deep, cols), jnp.float32)] * 3
        + [pltpu.VMEM((deep, cols), jnp.int32), pltpu.VMEM((rows, cols), jnp.int32)]
        + [pltpu.VMEM((dirs, deep, cols), jnp.bfloat16)] * 3
        + [
            pltpu.VMEM((dirs * rows, cols), jnp.float32),
            pltpu.SemaphoreType.DMA((6,)),
            pltpu.SemaphoreType.DMA((3, n_dep)),
        ],
        compiler_params=params,
        name="transport",
    )(
        *(
            pltpu.with_memory_space_constraint(x, pltpu.HBM)
            for x in (*base, line_label, island_label, *moving)
        )
    )
    arrived = exchange(small, "lat", None, 1)
    arrived, leaving = lax.optimization_barrier((arrived, rest))
    handed = exchange(leaving, "lat", None, 1)
    two = shape(2, 2 * share + 8, cols)
    near, far = call(core_kernel, "core", (two, two), small, arrived)
    blocks = call(
        merge_kernel, "merge", [shape(2, share * rows, cols)] * (n_dep - 1), rest, handed
    )
    blocks = [exchange(block, "dep", 0, s + 1) for s, block in enumerate(blocks)]
    first, second = call(depth_kernel, "depth", (full, full), *blocks)
    second = exchange(second, "lat", None, 1)
    half = shape(2 * share + 8, cols)
    kept, out = call(far_kernel, "far", (half, half), near, exchange(far, "dep", 1, 2))
    total, small = call(
        near_kernel, "near", (shape(share, cols), shape(share + 8, cols)), kept,
        exchange(out, "dep", 1, 1),
    )
    before = []
    bit = 2
    while bit < n_lat:
        *before, small = call(
            functools.partial(lat_kernel, bit), "bands",
            (shape(share, cols), shape(share + 8, cols)),
            small, exchange(small, "lat", 1, bit), *before,
        )
        bit *= 2
    bit = 1
    while 2 * bit < n_lon:
        small = small + exchange(small, "lon", 1, bit)
        bit *= 2
    small = call(
        lon_kernel, "lines", shape(share + 8, cols), small, exchange(small, "lon", 1, bit), *before
    )
    return call(
        stream_kernel, "stream", shape(share, rows, cols),
        own, first, second, small, exchange(small, "lat", None, 1), total, island,
    )


def solution(mesh):
    return jax.shard_map(
        shards,
        mesh=mesh,
        in_specs=(
            P("dep", "lat", "lon"),
            P("dep", "lat", "lon"),
            P("dep", "lat", "lon"),
            P(None, "dep", "lat", "lon"),
            P(None, "dep", "lat", "lon"),
            P(None, "dep", "lat", "lon"),
            P("dep", "lat", "lon"),
            P("lat", "lon"),
            P("lat", "lon"),
        ),
        out_specs=P("dep", "lat", "lon"),
        check_vma=False,
    )
```

```python
import functools
import math

import jax
import jax.numpy as jnp
from jax import lax
from jax.experimental import pallas as pl
from jax.experimental.pallas import tpu as pltpu
from jax.sharding import PartitionSpec as P

NISL = 32
VMEM_BYTES = 16 * 1024 * 1024
LARGE = 225_000_000
PARTS = (0.0, 0.4, 0.4, 0.2, 2.0)


def transport_kernel(
    east_scale, north_scale, thick_hbm, zonal_hbm, merid_hbm, sea_hbm, line_hbm, island_hbm, dz_hbm,
    dm_hbm, dt_hbm, *refs,
):
    (*east, small, island, thick, zonal, merid, sea, line, dz, dm, dt, north, base_sems, sems) = refs
    n_dep = len(east)
    mine = lax.axis_index("dep")
    share = dz.shape[0] // n_dep
    rows, cols = line.shape
    deep = dz.shape[1]
    base = [
        pltpu.make_async_copy(src, dst, base_sems.at[k])
        for k, (src, dst) in enumerate(
            (
                (thick_hbm, thick), (zonal_hbm, zonal), (merid_hbm, merid), (sea_hbm, sea),
                (line_hbm, line), (island_hbm, island),
            )
        )
    ]

    def copies(b):
        part = pl.ds((mine ^ b) * share, share)
        return [
            pltpu.make_async_copy(src.at[part], dst.at[part], sems.at[k, b])
            for k, (src, dst) in enumerate(((dz_hbm, dz), (dm_hbm, dm), (dt_hbm, dt)))
        ]

    for copy in base:
        copy.start()
    for b in reversed(range(n_dep)):
        for copy in copies(b):
            copy.start()
    for copy in base:
        copy.wait()
    wet = sea[...].astype(jnp.float32)
    east_thick = wet * thick[...] * east_scale
    east_base = wet * zonal[...] * east_scale
    north_thick = wet * thick[...] * north_scale
    north_base = wet * merid[...] * north_scale

    def levels(value):
        return jnp.sum(value.reshape(deep // rows, rows, cols), axis=0)

    for b in reversed(range(n_dep)):
        for copy in copies(b):
            copy.wait()
        for d in range(share):
            at = (mine ^ b) * share + d
            z, m, t = (ref[at].astype(jnp.float32) for ref in (dz, dm, dt))
            value = levels(z * east_thick + t * east_base)
            east[b][d * rows : (d + 1) * rows, :] = value
            small[b, d : d + 1, :] = jnp.sum(value, axis=0, keepdims=True)
            at = (b * share + d) * rows
            north[at : at + rows, :] = levels(m * north_thick + t * north_base)
    labels = lax.broadcasted_iota(jnp.int32, (NISL, cols), 0) + 1
    hot = jnp.concatenate(
        [(line[i : i + 1, :] == labels).astype(jnp.bfloat16) for i in range(rows)], axis=1
    )
    dirs = n_dep * share
    value = jnp.concatenate([north[pl.ds(i, dirs, stride=rows), :] for i in range(rows)], axis=1)
    high = value.astype(jnp.bfloat16)
    low = (value - high.astype(jnp.float32)).astype(jnp.bfloat16)
    sums = lax.dot_general(
        jnp.concatenate([high, low], axis=0), hot, (((1,), (1,)), ((), ())),
        preferred_element_type=jnp.float32,
    )
    sums = sums[:dirs] + sums[dirs:]
    quarter = share // 4
    lines = [
        jnp.concatenate(
            [sums[b * share + g * quarter : b * share + (g + 1) * quarter] for g in range(4)],
            axis=1,
        )
        for b in range(n_dep)
    ]
    for b in range(n_dep):
        small[b, share : share + quarter, :] = lines[b]
        small[b, share + quarter :, :] = jnp.zeros((8 - quarter, cols), jnp.float32)


def stage(part):
    return pl.CostEstimate(flops=int(part * LARGE), bytes_accessed=0, transcendentals=0)


def core_kernel(small, arrived, near, far):
    share = small.shape[1] - 8
    odd = (lax.axis_index("lat") & 1) != 0
    for k in range(2):
        for out, at in ((near, k), (far, 2 + k)):
            out[k, :share, :] = jnp.where(odd, arrived[at, :share, :], small[at, :share, :])
            out[k, share:, :] = small[at] + arrived[at]


def far_kernel(near, arrived, own, out):
    own[...] = near[0] + arrived[0]
    out[...] = near[1] + arrived[1]


def near_kernel(own, arrived, first, out):
    value = own[...] + arrived[...]
    share = first.shape[0]
    odd = (lax.axis_index("lat") & 1) != 0
    first[...] = jnp.where(odd, value[:share], 0.0)
    out[...] = value[share:]


def lat_kernel(bit, small, arrived, before, *refs):
    south, out = refs
    share = before.shape[0]
    part = jnp.where((lax.axis_index("lat") & bit) != 0, arrived[:share, :], 0.0)
    south[...] = before[...] + part
    out[...] = small[...] + arrived[...]


def lines_kernel(small, arrived, first, second, third, out, total):
    out[...] = small[...] + arrived[...]
    total[...] = first[...] + second[...] + third[...]


def stream_kernel(east, more, before, small, island, out):
    share, rows, cols = out.shape
    running = (east[...] + more[...]).reshape(share, rows, cols)
    row = lax.broadcasted_iota(jnp.int32, (share, rows, cols), 1)
    step = 1
    while step < rows:
        running = running + jnp.where(row >= step, pltpu.roll(running, step, 1), 0.0)
        step *= 2
    circ = small[share:, :]
    label = island[...]
    some = label > 0
    place = jnp.maximum(label - 1, 0)
    for d in range(share):
        g, r = d // 4, d % 4
        constant = jnp.take_along_axis(
            jnp.broadcast_to(circ[r : r + 1, :], (rows, cols)), place + g * NISL, axis=1
        )
        out[d] = running[d] + before[d : d + 1, :] + jnp.where(some, constant, 0.0)


def swap(value, axis, bit):
    n_lat, count = lax.axis_size("lat"), lax.axis_size(axis)
    if axis == "lat":
        return lax.ppermute(value, "lat", [(i, i ^ bit ^ 1) for i in range(n_lat)])
    return lax.ppermute(
        value,
        ("lat", axis),
        [(i * count + j, (i ^ 1) * count + (j ^ bit)) for i in range(n_lat) for j in range(count)],
    )


def shards(thick, zonal, merid, d_zonal, d_merid, d_thick, land_sea, line_label, island_label):
    dirs, levels, rows, cols = d_zonal.shape
    n_lat = lax.axis_size("lat")
    n_lon = lax.axis_size("lon")
    n_dep = lax.axis_size("dep")
    share = dirs // n_dep
    level_scale = 1.0 / math.sqrt(levels * n_dep)
    row_scale = 1.0 / math.sqrt(rows * n_lat)
    line_scale = 1.0 / math.sqrt(rows * n_lat * cols * n_lon / (NISL + 1))
    deep = levels * rows
    base = [x.reshape(deep, cols) for x in (thick, zonal, merid, land_sea)]
    moving = [x.reshape(dirs, deep, cols) for x in (d_zonal, d_merid, d_thick)]
    vmem = pl.BlockSpec(memory_space=pltpu.VMEM)
    hbm = pl.BlockSpec(memory_space=pltpu.HBM)
    params = pltpu.CompilerParams(vmem_limit_bytes=VMEM_BYTES)

    def call(kernel, name, out_shape, *operands, part=0.0):
        return pl.pallas_call(
            kernel,
            out_shape=out_shape,
            in_specs=[vmem] * len(operands),
            out_specs=jax.tree.map(lambda _: vmem, out_shape),
            compiler_params=params,
            cost_estimate=stage(part),
            name=name,
        )(*operands)

    def shape(*sizes):
        return jax.ShapeDtypeStruct(sizes, jnp.float32)

    full = shape(share * rows, cols)
    *east, small, island = pl.pallas_call(
        functools.partial(transport_kernel, -level_scale * row_scale, level_scale * line_scale),
        out_shape=(
            *[full] * n_dep,
            shape(n_dep, share + 8, cols),
            jax.ShapeDtypeStruct((rows, cols), jnp.int32),
        ),
        in_specs=[hbm] * 9,
        out_specs=tuple([vmem] * (n_dep + 2)),
        scratch_shapes=[pltpu.VMEM((deep, cols), jnp.float32)] * 3
        + [pltpu.VMEM((deep, cols), jnp.int32), pltpu.VMEM((rows, cols), jnp.int32)]
        + [pltpu.VMEM((dirs, deep, cols), jnp.bfloat16)] * 3
        + [
            pltpu.VMEM((dirs * rows, cols), jnp.float32),
            pltpu.SemaphoreType.DMA((6,)),
            pltpu.SemaphoreType.DMA((3, n_dep)),
        ],
        compiler_params=params,
        name="transport",
    )(
        *(
            pltpu.with_memory_space_constraint(x, pltpu.HBM)
            for x in (*base, line_label, island_label, *moving)
        )
    )
    arrived = lax.ppermute(small, "lat", [(i, i ^ 1) for i in range(n_lat)])
    two = shape(2, 2 * share + 8, cols)
    near, far = call(core_kernel, "core", (two, two), small, arrived, part=PARTS[0])
    far, east[3], east[2] = lax.optimization_barrier((far, east[3], east[2]))
    for s in (3, 2):
        east[s] = lax.ppermute(east[s], "dep", [(i, i ^ s) for i in range(n_dep)])
    half = shape(2 * share + 8, cols)
    own, out = call(far_kernel, "far", (half, half), near, swap(far, "dep", 2), part=PARTS[1])
    before, small = call(
        near_kernel, "near", (shape(share, cols), shape(share + 8, cols)), own, swap(out, "dep", 1),
        part=PARTS[2],
    )
    small, east[1] = lax.optimization_barrier((small, east[1]))
    east[1] = lax.ppermute(east[1], "dep", [(i, i ^ 1) for i in range(n_dep)])
    bit = 2
    while bit < n_lat:
        before, small = call(
            functools.partial(lat_kernel, bit), "bands",
            (shape(share, cols), shape(share + 8, cols)),
            small, swap(small, "lat", bit), before, part=PARTS[3],
        )
        bit *= 2
    bit = 1
    while 2 * bit < n_lon:
        small = small + swap(small, "lon", bit)
        bit *= 2
    small, total = call(
        lines_kernel, "lines", (shape(share + 8, cols), full),
        small, swap(small, "lon", bit), east[0], east[3], east[2], part=PARTS[4],
    )
    return call(
        stream_kernel, "stream", shape(share, rows, cols),
        total, east[1], before, small, island,
    )


def solution(mesh):
    return jax.shard_map(
        shards,
        mesh=mesh,
        in_specs=(
            P("dep", "lat", "lon"),
            P("dep", "lat", "lon"),
            P("dep", "lat", "lon"),
            P(None, "dep", "lat", "lon"),
            P(None, "dep", "lat", "lon"),
            P(None, "dep", "lat", "lon"),
            P("dep", "lat", "lon"),
            P("lat", "lon"),
            P("lat", "lon"),
        ),
        out_specs=P("dep", "lat", "lon"),
        check_vma=False,
    )
```

```python
import functools
import math

import jax
import jax.numpy as jnp
from jax import lax
from jax.experimental import pallas as pl
from jax.experimental.pallas import tpu as pltpu
from jax.sharding import PartitionSpec as P

NISL = 32
VMEM_BYTES = 16 * 1024 * 1024
LARGE = 400_000_000
PARTS = (0.0, 0.4, 0.4, 0.4, 1.0)


def transport_kernel(
    east_scale, north_scale, thick_hbm, zonal_hbm, merid_hbm, sea_hbm, line_hbm, island_hbm, dz_hbm,
    dm_hbm, dt_hbm, *refs,
):
    (*east, small, island, thick, zonal, merid, sea, line, dz, dm, dt, north, base_sems, sems) = refs
    n_dep = len(east)
    mine = lax.axis_index("dep")
    share = dz.shape[0] // n_dep
    rows, cols = line.shape
    deep = dz.shape[1]
    base = [
        pltpu.make_async_copy(src, dst, base_sems.at[k])
        for k, (src, dst) in enumerate(
            (
                (thick_hbm, thick), (zonal_hbm, zonal), (merid_hbm, merid), (sea_hbm, sea),
                (line_hbm, line), (island_hbm, island),
            )
        )
    ]

    def copies(b):
        part = pl.ds((mine ^ b) * share, share)
        return [
            pltpu.make_async_copy(src.at[part], dst.at[part], sems.at[k, b])
            for k, (src, dst) in enumerate(((dz_hbm, dz), (dm_hbm, dm), (dt_hbm, dt)))
        ]

    for copy in base:
        copy.start()
    for b in reversed(range(n_dep)):
        for copy in copies(b):
            copy.start()
    for copy in base:
        copy.wait()
    wet = sea[...].astype(jnp.float32)
    east_thick = wet * thick[...] * east_scale
    east_base = wet * zonal[...] * east_scale
    north_thick = wet * thick[...] * north_scale
    north_base = wet * merid[...] * north_scale

    def levels(value):
        return jnp.sum(value.reshape(deep // rows, rows, cols), axis=0)

    for b in reversed(range(n_dep)):
        for copy in copies(b):
            copy.wait()
        for d in range(share):
            at = (mine ^ b) * share + d
            z, m, t = (ref[at].astype(jnp.float32) for ref in (dz, dm, dt))
            value = levels(z * east_thick + t * east_base)
            east[b][d * rows : (d + 1) * rows, :] = value
            small[b, d : d + 1, :] = jnp.sum(value, axis=0, keepdims=True)
            at = (b * share + d) * rows
            north[at : at + rows, :] = levels(m * north_thick + t * north_base)
    labels = lax.broadcasted_iota(jnp.int32, (NISL, cols), 0) + 1
    hot = jnp.concatenate(
        [(line[i : i + 1, :] == labels).astype(jnp.bfloat16) for i in range(rows)], axis=1
    )
    dirs = n_dep * share
    value = jnp.concatenate([north[pl.ds(i, dirs, stride=rows), :] for i in range(rows)], axis=1)
    high = value.astype(jnp.bfloat16)
    low = (value - high.astype(jnp.float32)).astype(jnp.bfloat16)
    sums = lax.dot_general(
        jnp.concatenate([high, low], axis=0), hot, (((1,), (1,)), ((), ())),
        preferred_element_type=jnp.float32,
    )
    sums = sums[:dirs] + sums[dirs:]
    quarter = share // 4
    lines = [
        jnp.concatenate(
            [sums[b * share + g * quarter : b * share + (g + 1) * quarter] for g in range(4)],
            axis=1,
        )
        for b in range(n_dep)
    ]
    for b in range(n_dep):
        small[b, share : share + quarter, :] = lines[b]
        small[b, share + quarter :, :] = jnp.zeros((8 - quarter, cols), jnp.float32)


def stage(part):
    return pl.CostEstimate(flops=int(part * LARGE), bytes_accessed=0, transcendentals=0)


def core_kernel(small, arrived, near, far):
    share = small.shape[1] - 8
    odd = (lax.axis_index("lat") & 1) != 0
    for k in range(2):
        for out, at in ((near, k), (far, 2 + k)):
            out[k, :share, :] = jnp.where(odd, arrived[at, :share, :], small[at, :share, :])
            out[k, share:, :] = small[at] + arrived[at]


def far_kernel(near, arrived, own, out):
    own[...] = near[0] + arrived[0]
    out[...] = near[1] + arrived[1]


def near_kernel(own, arrived, first, out):
    value = own[...] + arrived[...]
    share = first.shape[0]
    odd = (lax.axis_index("lat") & 1) != 0
    first[...] = jnp.where(odd, value[:share], 0.0)
    out[...] = value[share:]


def lat_kernel(bit, small, arrived, before, *refs):
    south, out = refs
    share = before.shape[0]
    part = jnp.where((lax.axis_index("lat") & bit) != 0, arrived[:share, :], 0.0)
    south[...] = before[...] + part
    out[...] = small[...] + arrived[...]


def lines_kernel(small, arrived, first, second, third, out, total):
    out[...] = small[...] + arrived[...]
    total[...] = first[...] + second[...] + third[...]


def stream_kernel(east, more, before, small, island, out):
    share, rows, cols = out.shape
    running = (east[...] + more[...]).reshape(share, rows, cols)
    row = lax.broadcasted_iota(jnp.int32, (share, rows, cols), 1)
    step = 1
    while step < rows:
        running = running + jnp.where(row >= step, pltpu.roll(running, step, 1), 0.0)
        step *= 2
    circ = small[share:, :]
    label = island[...]
    some = label > 0
    place = jnp.maximum(label - 1, 0)
    for d in range(share):
        g, r = d // 4, d % 4
        constant = jnp.take_along_axis(
            jnp.broadcast_to(circ[r : r + 1, :], (rows, cols)), place + g * NISL, axis=1
        )
        out[d] = running[d] + before[d : d + 1, :] + jnp.where(some, constant, 0.0)


def swap(value, axis, bit):
    n_lat, count = lax.axis_size("lat"), lax.axis_size(axis)
    if axis == "lat":
        return lax.ppermute(value, "lat", [(i, i ^ bit ^ 1) for i in range(n_lat)])
    return lax.ppermute(
        value,
        ("lat", axis),
        [(i * count + j, (i ^ 1) * count + (j ^ bit)) for i in range(n_lat) for j in range(count)],
    )


def shards(thick, zonal, merid, d_zonal, d_merid, d_thick, land_sea, line_label, island_label):
    dirs, levels, rows, cols = d_zonal.shape
    n_lat = lax.axis_size("lat")
    n_lon = lax.axis_size("lon")
    n_dep = lax.axis_size("dep")
    share = dirs // n_dep
    level_scale = 1.0 / math.sqrt(levels * n_dep)
    row_scale = 1.0 / math.sqrt(rows * n_lat)
    line_scale = 1.0 / math.sqrt(rows * n_lat * cols * n_lon / (NISL + 1))
    deep = levels * rows
    base = [x.reshape(deep, cols) for x in (thick, zonal, merid, land_sea)]
    moving = [x.reshape(dirs, deep, cols) for x in (d_zonal, d_merid, d_thick)]
    vmem = pl.BlockSpec(memory_space=pltpu.VMEM)
    hbm = pl.BlockSpec(memory_space=pltpu.HBM)
    params = pltpu.CompilerParams(vmem_limit_bytes=VMEM_BYTES)

    def call(kernel, name, out_shape, *operands, part=0.0):
        return pl.pallas_call(
            kernel,
            out_shape=out_shape,
            in_specs=[vmem] * len(operands),
            out_specs=jax.tree.map(lambda _: vmem, out_shape),
            compiler_params=params,
            cost_estimate=stage(part),
            name=name,
        )(*operands)

    def shape(*sizes):
        return jax.ShapeDtypeStruct(sizes, jnp.float32)

    full = shape(share * rows, cols)
    *east, small, island = pl.pallas_call(
        functools.partial(transport_kernel, -level_scale * row_scale, level_scale * line_scale),
        out_shape=(
            *[full] * n_dep,
            shape(n_dep, share + 8, cols),
            jax.ShapeDtypeStruct((rows, cols), jnp.int32),
        ),
        in_specs=[hbm] * 9,
        out_specs=tuple([vmem] * (n_dep + 2)),
        scratch_shapes=[pltpu.VMEM((deep, cols), jnp.float32)] * 3
        + [pltpu.VMEM((deep, cols), jnp.int32), pltpu.VMEM((rows, cols), jnp.int32)]
        + [pltpu.VMEM((dirs, deep, cols), jnp.bfloat16)] * 3
        + [
            pltpu.VMEM((dirs * rows, cols), jnp.float32),
            pltpu.SemaphoreType.DMA((6,)),
            pltpu.SemaphoreType.DMA((3, n_dep)),
        ],
        compiler_params=params,
        name="transport",
    )(
        *(
            pltpu.with_memory_space_constraint(x, pltpu.HBM)
            for x in (*base, line_label, island_label, *moving)
        )
    )
    arrived = lax.ppermute(small, "lat", [(i, i ^ 1) for i in range(n_lat)])
    two = shape(2, 2 * share + 8, cols)
    near, far = call(core_kernel, "core", (two, two), small, arrived, part=PARTS[0])
    far, east[3], east[2] = lax.optimization_barrier((far, east[3], east[2]))
    for s in (3, 2):
        east[s] = lax.ppermute(east[s], "dep", [(i, i ^ s) for i in range(n_dep)])
    half = shape(2 * share + 8, cols)
    own, out = call(far_kernel, "far", (half, half), near, swap(far, "dep", 2), part=PARTS[1])
    before, small = call(
        near_kernel, "near", (shape(share, cols), shape(share + 8, cols)), own, swap(out, "dep", 1),
        part=PARTS[2],
    )
    small, east[1] = lax.optimization_barrier((small, east[1]))
    east[1] = lax.ppermute(east[1], "dep", [(i, i ^ 1) for i in range(n_dep)])
    bit = 2
    while bit < n_lat:
        before, small = call(
            functools.partial(lat_kernel, bit), "bands",
            (shape(share, cols), shape(share + 8, cols)),
            small, swap(small, "lat", bit), before, part=PARTS[3],
        )
        bit *= 2
    bit = 1
    while 2 * bit < n_lon:
        small = small + swap(small, "lon", bit)
        bit *= 2
    small, total = call(
        lines_kernel, "lines", (shape(share + 8, cols), full),
        small, swap(small, "lon", bit), east[0], east[3], east[2], part=PARTS[4],
    )
    return call(
        stream_kernel, "stream", shape(share, rows, cols),
        total, east[1], before, small, island,
    )


def solution(mesh):
    return jax.shard_map(
        shards,
        mesh=mesh,
        in_specs=(
            P("dep", "lat", "lon"),
            P("dep", "lat", "lon"),
            P("dep", "lat", "lon"),
            P(None, "dep", "lat", "lon"),
            P(None, "dep", "lat", "lon"),
            P(None, "dep", "lat", "lon"),
            P("dep", "lat", "lon"),
            P("lat", "lon"),
            P("lat", "lon"),
        ),
        out_specs=P("dep", "lat", "lon"),
        check_vma=False,
    )
```

```python
import functools
import math

import jax
import jax.numpy as jnp
from jax import lax
from jax.experimental import pallas as pl
from jax.experimental.pallas import tpu as pltpu
from jax.sharding import PartitionSpec as P

NISL = 32
VMEM_BYTES = 16 * 1024 * 1024
LARGE = 400_000_000
PARTS = (0.0, 0.4, 0.4, 0.4, 1.0)


def transport_kernel(
    east_scale, north_scale, thick_hbm, zonal_hbm, merid_hbm, sea_hbm, line_hbm, island_hbm, dz_hbm,
    dm_hbm, dt_hbm, *refs,
):
    (*east, small, island, thick, zonal, merid, sea, line, dz, dm, dt, north, base_sems, sems) = refs
    n_dep = len(east)
    mine = lax.axis_index("dep")
    share = dz.shape[0] // n_dep
    rows, cols = line.shape
    deep = dz.shape[1]
    base = [
        pltpu.make_async_copy(src, dst, base_sems.at[k])
        for k, (src, dst) in enumerate(
            (
                (thick_hbm, thick), (zonal_hbm, zonal), (merid_hbm, merid), (sea_hbm, sea),
                (line_hbm, line), (island_hbm, island),
            )
        )
    ]

    def copies(b):
        part = pl.ds((mine ^ b) * share, share)
        return [
            pltpu.make_async_copy(src.at[part], dst.at[part], sems.at[k, b])
            for k, (src, dst) in enumerate(((dz_hbm, dz), (dm_hbm, dm), (dt_hbm, dt)))
        ]

    for copy in base:
        copy.start()
    for b in reversed(range(n_dep)):
        for copy in copies(b):
            copy.start()
    for copy in base:
        copy.wait()
    wet = sea[...].astype(jnp.float32)
    east_thick = wet * thick[...] * east_scale
    east_base = wet * zonal[...] * east_scale
    north_thick = wet * thick[...] * north_scale
    north_base = wet * merid[...] * north_scale

    def levels(value):
        return jnp.sum(value.reshape(deep // rows, rows, cols), axis=0)

    for b in reversed(range(n_dep)):
        for copy in copies(b):
            copy.wait()
        for d in range(share):
            at = (mine ^ b) * share + d
            z, m, t = (ref[at].astype(jnp.float32) for ref in (dz, dm, dt))
            value = levels(z * east_thick + t * east_base)
            east[b][d * rows : (d + 1) * rows, :] = value
            small[b, d : d + 1, :] = jnp.sum(value, axis=0, keepdims=True)
            at = (b * share + d) * rows
            north[at : at + rows, :] = levels(m * north_thick + t * north_base)
    labels = lax.broadcasted_iota(jnp.int32, (NISL, cols), 0) + 1
    hot = jnp.concatenate(
        [(line[i : i + 1, :] == labels).astype(jnp.bfloat16) for i in range(rows)], axis=1
    )
    dirs = n_dep * share
    value = jnp.concatenate([north[pl.ds(i, dirs, stride=rows), :] for i in range(rows)], axis=1)
    high = value.astype(jnp.bfloat16)
    low = (value - high.astype(jnp.float32)).astype(jnp.bfloat16)
    sums = lax.dot_general(
        jnp.concatenate([high, low], axis=0), hot, (((1,), (1,)), ((), ())),
        preferred_element_type=jnp.float32,
    )
    sums = sums[:dirs] + sums[dirs:]
    quarter = share // 4
    lines = [
        jnp.concatenate(
            [sums[b * share + g * quarter : b * share + (g + 1) * quarter] for g in range(4)],
            axis=1,
        )
        for b in range(n_dep)
    ]
    for b in range(n_dep):
        small[b, share : share + quarter, :] = lines[b]
        small[b, share + quarter :, :] = jnp.zeros((8 - quarter, cols), jnp.float32)


def stage(part):
    return pl.CostEstimate(flops=int(part * LARGE), bytes_accessed=0, transcendentals=0)


def core_kernel(small, arrived, near, far):
    share = small.shape[1] - 8
    odd = (lax.axis_index("lat") & 1) != 0
    for k in range(2):
        for out, at in ((near, 2 * k), (far, 2 * k + 1)):
            out[k, :share, :] = jnp.where(odd, arrived[at, :share, :], small[at, :share, :])
            out[k, share:, :] = small[at] + arrived[at]


def far_kernel(near, arrived, own, out):
    own[...] = near[0] + arrived[0]
    out[...] = near[1] + arrived[1]


def near_kernel(own, arrived, first, out):
    value = own[...] + arrived[...]
    share = first.shape[0]
    odd = (lax.axis_index("lat") & 1) != 0
    first[...] = jnp.where(odd, value[:share], 0.0)
    out[...] = value[share:]


def lat_kernel(bit, small, arrived, before, *refs):
    south, out = refs
    share = before.shape[0]
    part = jnp.where((lax.axis_index("lat") & bit) != 0, arrived[:share, :], 0.0)
    south[...] = before[...] + part
    out[...] = small[...] + arrived[...]


def lines_kernel(small, arrived, first, second, third, out, total):
    out[...] = small[...] + arrived[...]
    total[...] = first[...] + second[...] + third[...]


def stream_kernel(east, more, before, small, island, out):
    share, rows, cols = out.shape
    running = (east[...] + more[...]).reshape(share, rows, cols)
    row = lax.broadcasted_iota(jnp.int32, (share, rows, cols), 1)
    step = 1
    while step < rows:
        running = running + jnp.where(row >= step, pltpu.roll(running, step, 1), 0.0)
        step *= 2
    circ = small[share:, :]
    label = island[...]
    some = label > 0
    place = jnp.maximum(label - 1, 0)
    for d in range(share):
        g, r = d // 4, d % 4
        constant = jnp.take_along_axis(
            jnp.broadcast_to(circ[r : r + 1, :], (rows, cols)), place + g * NISL, axis=1
        )
        out[d] = running[d] + before[d : d + 1, :] + jnp.where(some, constant, 0.0)


def swap(value, axis, bit):
    n_lat, count = lax.axis_size("lat"), lax.axis_size(axis)
    if axis == "lat":
        return lax.ppermute(value, "lat", [(i, i ^ bit ^ 1) for i in range(n_lat)])
    return lax.ppermute(
        value,
        ("lat", axis),
        [(i * count + j, (i ^ 1) * count + (j ^ bit)) for i in range(n_lat) for j in range(count)],
    )


def shards(thick, zonal, merid, d_zonal, d_merid, d_thick, land_sea, line_label, island_label):
    dirs, levels, rows, cols = d_zonal.shape
    n_lat = lax.axis_size("lat")
    n_lon = lax.axis_size("lon")
    n_dep = lax.axis_size("dep")
    share = dirs // n_dep
    level_scale = 1.0 / math.sqrt(levels * n_dep)
    row_scale = 1.0 / math.sqrt(rows * n_lat)
    line_scale = 1.0 / math.sqrt(rows * n_lat * cols * n_lon / (NISL + 1))
    deep = levels * rows
    base = [x.reshape(deep, cols) for x in (thick, zonal, merid, land_sea)]
    moving = [x.reshape(dirs, deep, cols) for x in (d_zonal, d_merid, d_thick)]
    vmem = pl.BlockSpec(memory_space=pltpu.VMEM)
    hbm = pl.BlockSpec(memory_space=pltpu.HBM)
    params = pltpu.CompilerParams(vmem_limit_bytes=VMEM_BYTES)

    def call(kernel, name, out_shape, *operands, part=0.0):
        return pl.pallas_call(
            kernel,
            out_shape=out_shape,
            in_specs=[vmem] * len(operands),
            out_specs=jax.tree.map(lambda _: vmem, out_shape),
            compiler_params=params,
            cost_estimate=stage(part),
            name=name,
        )(*operands)

    def shape(*sizes):
        return jax.ShapeDtypeStruct(sizes, jnp.float32)

    full = shape(share * rows, cols)
    *east, small, island = pl.pallas_call(
        functools.partial(transport_kernel, -level_scale * row_scale, level_scale * line_scale),
        out_shape=(
            *[full] * n_dep,
            shape(n_dep, share + 8, cols),
            jax.ShapeDtypeStruct((rows, cols), jnp.int32),
        ),
        in_specs=[hbm] * 9,
        out_specs=tuple([vmem] * (n_dep + 2)),
        scratch_shapes=[pltpu.VMEM((deep, cols), jnp.float32)] * 3
        + [pltpu.VMEM((deep, cols), jnp.int32), pltpu.VMEM((rows, cols), jnp.int32)]
        + [pltpu.VMEM((dirs, deep, cols), jnp.bfloat16)] * 3
        + [
            pltpu.VMEM((dirs * rows, cols), jnp.float32),
            pltpu.SemaphoreType.DMA((6,)),
            pltpu.SemaphoreType.DMA((3, n_dep)),
        ],
        compiler_params=params,
        name="transport",
    )(
        *(
            pltpu.with_memory_space_constraint(x, pltpu.HBM)
            for x in (*base, line_label, island_label, *moving)
        )
    )
    arrived = lax.ppermute(small, "lat", [(i, i ^ 1) for i in range(n_lat)])
    two = shape(2, 2 * share + 8, cols)
    near, far = call(core_kernel, "core", (two, two), small, arrived, part=PARTS[0])
    far, east[3], east[2] = lax.optimization_barrier((far, east[3], east[2]))
    for s in (3, 2):
        east[s] = lax.ppermute(east[s], "dep", [(i, i ^ s) for i in range(n_dep)])
    half = shape(2 * share + 8, cols)
    own, out = call(far_kernel, "far", (half, half), near, swap(far, "dep", 1), part=PARTS[1])
    before, small = call(
        near_kernel, "near", (shape(share, cols), shape(share + 8, cols)), own, swap(out, "dep", 2),
        part=PARTS[2],
    )
    small, east[1] = lax.optimization_barrier((small, east[1]))
    east[1] = lax.ppermute(east[1], "dep", [(i, i ^ 1) for i in range(n_dep)])
    bit = 2
    while bit < n_lat:
        before, small = call(
            functools.partial(lat_kernel, bit), "bands",
            (shape(share, cols), shape(share + 8, cols)),
            small, swap(small, "lat", bit), before, part=PARTS[3],
        )
        bit *= 2
    bit = 1
    while 2 * bit < n_lon:
        small = small + swap(small, "lon", bit)
        bit *= 2
    small, total = call(
        lines_kernel, "lines", (shape(share + 8, cols), full),
        small, swap(small, "lon", bit), east[0], east[3], east[2], part=PARTS[4],
    )
    return call(
        stream_kernel, "stream", shape(share, rows, cols),
        total, east[1], before, small, island,
    )


def solution(mesh):
    return jax.shard_map(
        shards,
        mesh=mesh,
        in_specs=(
            P("dep", "lat", "lon"),
            P("dep", "lat", "lon"),
            P("dep", "lat", "lon"),
            P(None, "dep", "lat", "lon"),
            P(None, "dep", "lat", "lon"),
            P(None, "dep", "lat", "lon"),
            P("dep", "lat", "lon"),
            P("lat", "lon"),
            P("lat", "lon"),
        ),
        out_specs=P("dep", "lat", "lon"),
        check_vma=False,
    )
```

```python
import functools
import math

import jax
import jax.numpy as jnp
from jax import lax
from jax.experimental import pallas as pl
from jax.experimental.pallas import tpu as pltpu
from jax.sharding import PartitionSpec as P

NISL = 32
VMEM_BYTES = 16 * 1024 * 1024
LARGE = 300_000_000
PARTS = (0.0, 2.0, 0.8, 0.4, 0.4)


def transport_kernel(
    east_scale, north_scale, thick_hbm, zonal_hbm, merid_hbm, sea_hbm, line_hbm, island_hbm, dz_hbm,
    dm_hbm, dt_hbm, *refs,
):
    (*east, small, island, thick, zonal, merid, sea, line, dz, dm, dt, north, halves, base_sems, sems) = refs
    n_dep = len(east)
    mine = lax.axis_index("dep")
    share = dz.shape[0] // n_dep
    rows, cols = line.shape
    deep = dz.shape[1]
    base = [
        pltpu.make_async_copy(src, dst, base_sems.at[k])
        for k, (src, dst) in enumerate(
            (
                (thick_hbm, thick), (zonal_hbm, zonal), (merid_hbm, merid), (sea_hbm, sea),
                (line_hbm, line), (island_hbm, island),
            )
        )
    ]

    def copies(b):
        part = pl.ds((mine ^ b) * share, share)
        return [
            pltpu.make_async_copy(src.at[part], dst.at[part], sems.at[k, b])
            for k, (src, dst) in enumerate(((dz_hbm, dz), (dm_hbm, dm), (dt_hbm, dt)))
        ]

    for copy in base:
        copy.start()
    for b in reversed(range(n_dep)):
        for copy in copies(b):
            copy.start()
    for copy in base:
        copy.wait()
    wet = sea[...].astype(jnp.float32)
    east_thick = wet * thick[...] * east_scale
    east_base = wet * zonal[...] * east_scale
    north_thick = wet * thick[...] * north_scale
    north_base = wet * merid[...] * north_scale

    def levels(value):
        return jnp.sum(value.reshape(deep // rows, rows, cols), axis=0)

    labels = lax.broadcasted_iota(jnp.int32, (NISL, cols), 0) + 1
    hot = jnp.concatenate(
        [(line[i : i + 1, :] == labels).astype(jnp.bfloat16) for i in range(rows)], axis=1
    )
    dirs = n_dep * share
    for b in reversed(range(n_dep)):
        for copy in copies(b):
            copy.wait()
        for d in range(share):
            at = (mine ^ b) * share + d
            z, m, t = (ref[at].astype(jnp.float32) for ref in (dz, dm, dt))
            part = slice(d * rows, (d + 1) * rows)
            east[b][part, :] = levels(z * east_thick + t * east_base)
            north[part, :] = levels(m * north_thick + t * north_base)
        totals = east[b][pl.ds(0, share, stride=rows), :]
        for i in range(1, rows):
            totals = totals + east[b][pl.ds(i, share, stride=rows), :]
        small[b, :share, :] = totals
        for i in range(rows):
            value = north[pl.ds(i, share, stride=rows), :]
            high = value.astype(jnp.bfloat16)
            low = (value - high.astype(jnp.float32)).astype(jnp.bfloat16)
            halves[b * share : (b + 1) * share, i * cols : (i + 1) * cols] = high
            halves[dirs + b * share : dirs + (b + 1) * share, i * cols : (i + 1) * cols] = low
    sums = lax.dot_general(
        halves[...], hot, (((1,), (1,)), ((), ())), preferred_element_type=jnp.float32
    )
    sums = sums[:dirs] + sums[dirs:]
    quarter = share // 4
    lines = [
        jnp.concatenate(
            [sums[b * share + g * quarter : b * share + (g + 1) * quarter] for g in range(4)],
            axis=1,
        )
        for b in range(n_dep)
    ]
    for b in range(n_dep):
        small[b, share : share + quarter, :] = lines[b]
        small[b, share + quarter :, :] = jnp.zeros((8 - quarter, cols), jnp.float32)


def stage(part):
    return pl.CostEstimate(flops=int(part * LARGE), bytes_accessed=0, transcendentals=0)


def core_kernel(small, arrived, near, far):
    share = small.shape[1] - 8
    odd = (lax.axis_index("lat") & 1) != 0
    for k in range(2):
        for out, at in ((near, 2 * k), (far, 2 * k + 1)):
            out[k, :share, :] = jnp.where(odd, arrived[at, :share, :], small[at, :share, :])
            out[k, share:, :] = small[at] + arrived[at]


def far_kernel(near, arrived, own, out):
    own[...] = near[0] + arrived[0]
    out[...] = near[1] + arrived[1]


def near_kernel(own, arrived, east, more, first, out, total):
    total[...] = east[...] + more[...]
    value = own[...] + arrived[...]
    share = first.shape[0]
    odd = (lax.axis_index("lat") & 1) != 0
    first[...] = jnp.where(odd, value[:share], 0.0)
    out[...] = value[share:]


def lat_kernel(bit, small, arrived, before, *refs):
    south, out = refs
    share = before.shape[0]
    part = jnp.where((lax.axis_index("lat") & bit) != 0, arrived[:share, :], 0.0)
    south[...] = before[...] + part
    out[...] = small[...] + arrived[...]


def lines_kernel(small, arrived, east, more, out, total):
    out[...] = small[...] + arrived[...]
    total[...] = east[...] + more[...]


def stream_kernel(east, more, before, small, island, out):
    share, rows, cols = out.shape
    running = (east[...] + more[...]).reshape(share, rows, cols)
    row = lax.broadcasted_iota(jnp.int32, (share, rows, cols), 1)
    step = 1
    while step < rows:
        running = running + jnp.where(row >= step, pltpu.roll(running, step, 1), 0.0)
        step *= 2
    circ = small[share:, :]
    label = island[...]
    some = label > 0
    place = jnp.maximum(label - 1, 0)
    for d in range(share):
        g, r = d // 4, d % 4
        constant = jnp.take_along_axis(
            jnp.broadcast_to(circ[r : r + 1, :], (rows, cols)), place + g * NISL, axis=1
        )
        out[d] = running[d] + before[d : d + 1, :] + jnp.where(some, constant, 0.0)


def swap(value, axis, bit):
    n_lat, count = lax.axis_size("lat"), lax.axis_size(axis)
    if axis == "lat":
        return lax.ppermute(value, "lat", [(i, i ^ bit ^ 1) for i in range(n_lat)])
    return lax.ppermute(
        value,
        ("lat", axis),
        [(i * count + j, (i ^ 1) * count + (j ^ bit)) for i in range(n_lat) for j in range(count)],
    )


def shards(thick, zonal, merid, d_zonal, d_merid, d_thick, land_sea, line_label, island_label):
    dirs, levels, rows, cols = d_zonal.shape
    n_lat = lax.axis_size("lat")
    n_lon = lax.axis_size("lon")
    n_dep = lax.axis_size("dep")
    share = dirs // n_dep
    level_scale = 1.0 / math.sqrt(levels * n_dep)
    row_scale = 1.0 / math.sqrt(rows * n_lat)
    line_scale = 1.0 / math.sqrt(rows * n_lat * cols * n_lon / (NISL + 1))
    deep = levels * rows
    base = [x.reshape(deep, cols) for x in (thick, zonal, merid, land_sea)]
    moving = [x.reshape(dirs, deep, cols) for x in (d_zonal, d_merid, d_thick)]
    vmem = pl.BlockSpec(memory_space=pltpu.VMEM)
    hbm = pl.BlockSpec(memory_space=pltpu.HBM)
    params = pltpu.CompilerParams(vmem_limit_bytes=VMEM_BYTES)

    def call(kernel, name, out_shape, *operands, part=0.0):
        return pl.pallas_call(
            kernel,
            out_shape=out_shape,
            in_specs=[vmem] * len(operands),
            out_specs=jax.tree.map(lambda _: vmem, out_shape),
            compiler_params=params,
            cost_estimate=stage(part),
            name=name,
        )(*operands)

    def shape(*sizes):
        return jax.ShapeDtypeStruct(sizes, jnp.float32)

    full = shape(share * rows, cols)
    *east, small, island = pl.pallas_call(
        functools.partial(transport_kernel, -level_scale * row_scale, level_scale * line_scale),
        out_shape=(
            *[full] * n_dep,
            shape(n_dep, share + 8, cols),
            jax.ShapeDtypeStruct((rows, cols), jnp.int32),
        ),
        in_specs=[hbm] * 9,
        out_specs=tuple([vmem] * (n_dep + 2)),
        scratch_shapes=[pltpu.VMEM((deep, cols), jnp.float32)] * 3
        + [pltpu.VMEM((deep, cols), jnp.int32), pltpu.VMEM((rows, cols), jnp.int32)]
        + [pltpu.VMEM((dirs, deep, cols), jnp.bfloat16)] * 3
        + [
            pltpu.VMEM((share * rows, cols), jnp.float32),
            pltpu.VMEM((2 * dirs, rows * cols), jnp.bfloat16),
            pltpu.SemaphoreType.DMA((6,)),
            pltpu.SemaphoreType.DMA((3, n_dep)),
        ],
        compiler_params=params,
        name="transport",
    )(
        *(
            pltpu.with_memory_space_constraint(x, pltpu.HBM)
            for x in (*base, line_label, island_label, *moving)
        )
    )
    arrived = lax.ppermute(small, "lat", [(i, i ^ 1) for i in range(n_lat)])
    two = shape(2, 2 * share + 8, cols)
    near, far = call(core_kernel, "core", (two, two), small, arrived, part=PARTS[0])
    far, east[1] = lax.optimization_barrier((far, east[1]))
    east[1] = lax.ppermute(east[1], "dep", [(i, i ^ 1) for i in range(n_dep)])
    half = shape(2 * share + 8, cols)
    own, out = call(far_kernel, "far", (half, half), near, swap(far, "dep", 1), part=PARTS[1])
    out, east[3], east[2] = lax.optimization_barrier((out, east[3], east[2]))
    for s in (3, 2):
        east[s] = lax.ppermute(east[s], "dep", [(i, i ^ s) for i in range(n_dep)])
    before, small, total = call(
        near_kernel, "near", (shape(share, cols), shape(share + 8, cols), full),
        own, swap(out, "dep", 2), east[0], east[1], part=PARTS[2],
    )
    bit = 2
    while bit < n_lat:
        before, small = call(
            functools.partial(lat_kernel, bit), "bands",
            (shape(share, cols), shape(share + 8, cols)),
            small, swap(small, "lat", bit), before, part=PARTS[3],
        )
        bit *= 2
    bit = 1
    while 2 * bit < n_lon:
        small = small + swap(small, "lon", bit)
        bit *= 2
    small, total = call(
        lines_kernel, "lines", (shape(share + 8, cols), full),
        small, swap(small, "lon", bit), total, east[3], part=PARTS[4],
    )
    return call(
        stream_kernel, "stream", shape(share, rows, cols),
        total, east[2], before, small, island,
    )


def solution(mesh):
    return jax.shard_map(
        shards,
        mesh=mesh,
        in_specs=(
            P("dep", "lat", "lon"),
            P("dep", "lat", "lon"),
            P("dep", "lat", "lon"),
            P(None, "dep", "lat", "lon"),
            P(None, "dep", "lat", "lon"),
            P(None, "dep", "lat", "lon"),
            P("dep", "lat", "lon"),
            P("lat", "lon"),
            P("lat", "lon"),
        ),
        out_specs=P("dep", "lat", "lon"),
        check_vma=False,
    )
```

```python
import functools
import math

import jax
import jax.numpy as jnp
from jax import lax
from jax.experimental import pallas as pl
from jax.experimental.pallas import tpu as pltpu
from jax.sharding import PartitionSpec as P

NISL = 32
VMEM_BYTES = 16 * 1024 * 1024
LARGE = 500_000_000
PARTS = (0.0, 2.0, 0.8, 0.4, 0.4)


def transport_kernel(
    east_scale, north_scale, thick_hbm, zonal_hbm, merid_hbm, sea_hbm, line_hbm, island_hbm, dz_hbm,
    dm_hbm, dt_hbm, *refs,
):
    (*east, small, island, thick, zonal, merid, sea, line, dz, dm, dt, north, base_sems, sems) = refs
    n_dep = len(east)
    mine = lax.axis_index("dep")
    share = dz.shape[0] // n_dep
    rows, cols = line.shape
    deep = dz.shape[1]
    base = [
        pltpu.make_async_copy(src, dst, base_sems.at[k])
        for k, (src, dst) in enumerate(
            (
                (thick_hbm, thick), (zonal_hbm, zonal), (merid_hbm, merid), (sea_hbm, sea),
                (line_hbm, line), (island_hbm, island),
            )
        )
    ]

    def copies(b):
        part = pl.ds((mine ^ b) * share, share)
        return [
            pltpu.make_async_copy(src.at[part], dst.at[part], sems.at[k, b])
            for k, (src, dst) in enumerate(((dz_hbm, dz), (dm_hbm, dm), (dt_hbm, dt)))
        ]

    for copy in base:
        copy.start()
    for b in reversed(range(n_dep)):
        for copy in copies(b):
            copy.start()
    for copy in base:
        copy.wait()
    wet = sea[...].astype(jnp.float32)
    east_thick = wet * thick[...] * east_scale
    east_base = wet * zonal[...] * east_scale
    north_thick = wet * thick[...] * north_scale
    north_base = wet * merid[...] * north_scale

    def levels(value):
        return jnp.sum(value.reshape(deep // rows, rows, cols), axis=0)

    labels = lax.broadcasted_iota(jnp.int32, (NISL, cols), 0) + 1
    hot = jnp.concatenate(
        [(line[i : i + 1, :] == labels).astype(jnp.bfloat16) for i in range(rows)], axis=1
    )
    for b in reversed(range(n_dep)):
        for copy in copies(b):
            copy.wait()
        for d in range(share):
            at = (mine ^ b) * share + d
            z, m, t = (ref[at].astype(jnp.float32) for ref in (dz, dm, dt))
            value = levels(z * east_thick + t * east_base)
            east[b][d * rows : (d + 1) * rows, :] = value
            small[b, d : d + 1, :] = jnp.sum(value, axis=0, keepdims=True)
            at = (b * share + d) * rows
            north[at : at + rows, :] = levels(m * north_thick + t * north_base)
    dirs = n_dep * share
    value = jnp.concatenate([north[pl.ds(i, dirs, stride=rows), :] for i in range(rows)], axis=1)
    high = value.astype(jnp.bfloat16)
    low = (value - high.astype(jnp.float32)).astype(jnp.bfloat16)
    sums = lax.dot_general(
        jnp.concatenate([high, low], axis=0), hot, (((1,), (1,)), ((), ())),
        preferred_element_type=jnp.float32,
    )
    sums = sums[:dirs] + sums[dirs:]
    quarter = share // 4
    lines = [
        jnp.concatenate(
            [sums[b * share + g * quarter : b * share + (g + 1) * quarter] for g in range(4)],
            axis=1,
        )
        for b in range(n_dep)
    ]
    for b in range(n_dep):
        small[b, share : share + quarter, :] = lines[b]
        small[b, share + quarter :, :] = jnp.zeros((8 - quarter, cols), jnp.float32)


def stage(part):
    return pl.CostEstimate(flops=int(part * LARGE), bytes_accessed=0, transcendentals=0)


def core_kernel(small, arrived, near, far):
    for k in range(2):
        near[k] = small[2 * k] + arrived[2 * k]
        far[k] = small[2 * k + 1] + arrived[2 * k + 1]


def blocks_kernel(arrived, *refs):
    count = len(refs) // 2
    for s, (east, out) in enumerate(zip(refs[:count], refs[count:])):
        size = east.shape[0]
        out[:size, :] = east[...]
        out[size:, :] = arrived[s, : out.shape[0] - size, :]


def far_kernel(near, arrived, own, out):
    own[...] = near[0] + arrived[0]
    out[...] = near[1] + arrived[1]


def near_kernel(own, arrived, east, more, out, total):
    out[...] = own[...] + arrived[...]
    total[...] = east[...] + more[...]


def lat_kernel(bit, small, arrived, *refs):
    *before, south, out = refs
    part = jnp.where((lax.axis_index("lat") & bit) != 0, arrived[: south.shape[0], :], 0.0)
    south[...] = before[0][...] + part if before else part
    out[...] = small[...] + arrived[...]


def lines_kernel(small, arrived, east, more, out, total):
    out[...] = small[...] + arrived[...]
    total[...] = east[...] + more[...]


def stream_kernel(east, more, before, small, island, out):
    share, rows, cols = out.shape
    odd = (lax.axis_index("lat") & 1) != 0
    value = east[...] + more[...]
    running = value[: share * rows].reshape(share, rows, cols)
    south = before[...] + jnp.where(odd, value[share * rows :], 0.0)
    row = lax.broadcasted_iota(jnp.int32, (share, rows, cols), 1)
    step = 1
    while step < rows:
        running = running + jnp.where(row >= step, pltpu.roll(running, step, 1), 0.0)
        step *= 2
    circ = small[share:, :]
    label = island[...]
    some = label > 0
    place = jnp.maximum(label - 1, 0)
    for d in range(share):
        g, r = d // 4, d % 4
        constant = jnp.take_along_axis(
            jnp.broadcast_to(circ[r : r + 1, :], (rows, cols)), place + g * NISL, axis=1
        )
        out[d] = running[d] + south[d : d + 1, :] + jnp.where(some, constant, 0.0)


def swap(value, axis, bit):
    n_lat, count = lax.axis_size("lat"), lax.axis_size(axis)
    if axis == "lat":
        return lax.ppermute(value, "lat", [(i, i ^ bit ^ 1) for i in range(n_lat)])
    return lax.ppermute(
        value,
        ("lat", axis),
        [(i * count + j, (i ^ 1) * count + (j ^ bit)) for i in range(n_lat) for j in range(count)],
    )


def shards(thick, zonal, merid, d_zonal, d_merid, d_thick, land_sea, line_label, island_label):
    dirs, levels, rows, cols = d_zonal.shape
    n_lat = lax.axis_size("lat")
    n_lon = lax.axis_size("lon")
    n_dep = lax.axis_size("dep")
    share = dirs // n_dep
    level_scale = 1.0 / math.sqrt(levels * n_dep)
    row_scale = 1.0 / math.sqrt(rows * n_lat)
    line_scale = 1.0 / math.sqrt(rows * n_lat * cols * n_lon / (NISL + 1))
    deep = levels * rows
    base = [x.reshape(deep, cols) for x in (thick, zonal, merid, land_sea)]
    moving = [x.reshape(dirs, deep, cols) for x in (d_zonal, d_merid, d_thick)]
    vmem = pl.BlockSpec(memory_space=pltpu.VMEM)
    hbm = pl.BlockSpec(memory_space=pltpu.HBM)
    params = pltpu.CompilerParams(vmem_limit_bytes=VMEM_BYTES)

    def call(kernel, name, out_shape, *operands, part=0.0):
        return pl.pallas_call(
            kernel,
            out_shape=out_shape,
            in_specs=[vmem] * len(operands),
            out_specs=jax.tree.map(lambda _: vmem, out_shape),
            compiler_params=params,
            cost_estimate=stage(part),
            name=name,
        )(*operands)

    def shape(*sizes):
        return jax.ShapeDtypeStruct(sizes, jnp.float32)

    full = shape(share * rows, cols)
    *east, small, island = pl.pallas_call(
        functools.partial(transport_kernel, -level_scale * row_scale, level_scale * line_scale),
        out_shape=(
            *[full] * n_dep,
            shape(n_dep, share + 8, cols),
            jax.ShapeDtypeStruct((rows, cols), jnp.int32),
        ),
        in_specs=[hbm] * 9,
        out_specs=tuple([vmem] * (n_dep + 2)),
        scratch_shapes=[pltpu.VMEM((deep, cols), jnp.float32)] * 3
        + [pltpu.VMEM((deep, cols), jnp.int32), pltpu.VMEM((rows, cols), jnp.int32)]
        + [pltpu.VMEM((dirs, deep, cols), jnp.bfloat16)] * 3
        + [
            pltpu.VMEM((dirs * rows, cols), jnp.float32),
            pltpu.SemaphoreType.DMA((6,)),
            pltpu.SemaphoreType.DMA((3, n_dep)),
        ],
        compiler_params=params,
        name="transport",
    )(
        *(
            pltpu.with_memory_space_constraint(x, pltpu.HBM)
            for x in (*base, line_label, island_label, *moving)
        )
    )
    arrived = lax.ppermute(small, "lat", [(i, i ^ 1) for i in range(n_lat)])
    two = shape(2, share + 8, cols)
    near, far = call(core_kernel, "core", (two, two), small, arrived, part=PARTS[0])
    full = shape(share * (rows + 1), cols)
    east = list(call(blocks_kernel, "blocks", [full] * n_dep, arrived, *east))
    far, east[1] = lax.optimization_barrier((far, east[1]))
    east[1] = lax.ppermute(east[1], "dep", [(i, i ^ 1) for i in range(n_dep)])
    half = shape(share + 8, cols)
    own, out = call(far_kernel, "far", (half, half), near, swap(far, "dep", 1), part=PARTS[1])
    out, east[3], east[2] = lax.optimization_barrier((out, east[3], east[2]))
    for s in (3, 2):
        east[s] = lax.ppermute(east[s], "dep", [(i, i ^ s) for i in range(n_dep)])
    small, total = call(
        near_kernel, "near", (half, full), own, swap(out, "dep", 2), east[0], east[1],
        part=PARTS[2],
    )
    before = []
    bit = 2
    while bit < n_lat:
        *before, small = call(
            functools.partial(lat_kernel, bit), "bands", (shape(share, cols), half),
            small, swap(small, "lat", bit), *before, part=PARTS[3],
        )
        bit *= 2
    bit = 1
    while 2 * bit < n_lon:
        small = small + swap(small, "lon", bit)
        bit *= 2
    small, total = call(
        lines_kernel, "lines", (shape(share + 8, cols), full),
        small, swap(small, "lon", bit), total, east[3], part=PARTS[4],
    )
    return call(
        stream_kernel, "stream", shape(share, rows, cols),
        total, east[2], *before, small, island,
    )


def solution(mesh):
    return jax.shard_map(
        shards,
        mesh=mesh,
        in_specs=(
            P("dep", "lat", "lon"),
            P("dep", "lat", "lon"),
            P("dep", "lat", "lon"),
            P(None, "dep", "lat", "lon"),
            P(None, "dep", "lat", "lon"),
            P(None, "dep", "lat", "lon"),
            P("dep", "lat", "lon"),
            P("lat", "lon"),
            P("lat", "lon"),
        ),
        out_specs=P("dep", "lat", "lon"),
        check_vma=False,
    )
```

```python
import functools
import math

import jax
import jax.numpy as jnp
from jax import lax
from jax.experimental import pallas as pl
from jax.experimental.pallas import tpu as pltpu
from jax.sharding import PartitionSpec as P

NISL = 32
VMEM_BYTES = 16 * 1024 * 1024
LARGE = 600_000_000
PARTS = (0.0, 3.0, 0.6, 0.2, 0.2)


def transport_kernel(
    east_scale, north_scale, thick_hbm, zonal_hbm, merid_hbm, sea_hbm, line_hbm, island_hbm, dz_hbm,
    dm_hbm, dt_hbm, *refs,
):
    (*east, small, island, thick, zonal, merid, sea, line, dz, dm, dt, north, base_sems, sems) = refs
    n_dep = len(east)
    mine = lax.axis_index("dep")
    share = dz.shape[0] // n_dep
    rows, cols = line.shape
    deep = dz.shape[1]
    base = [
        pltpu.make_async_copy(src, dst, base_sems.at[k])
        for k, (src, dst) in enumerate(
            (
                (thick_hbm, thick), (zonal_hbm, zonal), (merid_hbm, merid), (sea_hbm, sea),
                (line_hbm, line), (island_hbm, island),
            )
        )
    ]

    def copies(b):
        part = pl.ds((mine ^ b) * share, share)
        return [
            pltpu.make_async_copy(src.at[part], dst.at[part], sems.at[k, b])
            for k, (src, dst) in enumerate(((dz_hbm, dz), (dm_hbm, dm), (dt_hbm, dt)))
        ]

    for copy in base:
        copy.start()
    for b in reversed(range(n_dep)):
        for copy in copies(b):
            copy.start()
    for copy in base:
        copy.wait()
    wet = sea[...].astype(jnp.float32)
    east_thick = wet * thick[...] * east_scale
    east_base = wet * zonal[...] * east_scale
    north_thick = wet * thick[...] * north_scale
    north_base = wet * merid[...] * north_scale

    def levels(value):
        return jnp.sum(value.reshape(deep // rows, rows, cols), axis=0)

    for b in reversed(range(n_dep)):
        for copy in copies(b):
            copy.wait()
        for d in range(share):
            at = (mine ^ b) * share + d
            z, m, t = (ref[at].astype(jnp.float32) for ref in (dz, dm, dt))
            value = levels(z * east_thick + t * east_base)
            east[b][d * rows : (d + 1) * rows, :] = value
            small[b, d : d + 1, :] = jnp.sum(value, axis=0, keepdims=True)
            at = (b * share + d) * rows
            north[at : at + rows, :] = levels(m * north_thick + t * north_base)
    labels = lax.broadcasted_iota(jnp.int32, (NISL, cols), 0) + 1
    hot = jnp.concatenate(
        [(line[i : i + 1, :] == labels).astype(jnp.bfloat16) for i in range(rows)], axis=1
    )
    dirs = n_dep * share
    value = jnp.concatenate([north[pl.ds(i, dirs, stride=rows), :] for i in range(rows)], axis=1)
    high = value.astype(jnp.bfloat16)
    low = (value - high.astype(jnp.float32)).astype(jnp.bfloat16)
    sums = lax.dot_general(
        jnp.concatenate([high, low], axis=0), hot, (((1,), (1,)), ((), ())),
        preferred_element_type=jnp.float32,
    )
    sums = sums[:dirs] + sums[dirs:]
    quarter = share // 4
    lines = [
        jnp.concatenate(
            [sums[b * share + g * quarter : b * share + (g + 1) * quarter] for g in range(4)],
            axis=1,
        )
        for b in range(n_dep)
    ]
    for b in range(n_dep):
        small[b, share : share + quarter, :] = lines[b]
        small[b, share + quarter :, :] = jnp.zeros((8 - quarter, cols), jnp.float32)


def stage(part):
    return pl.CostEstimate(flops=int(part * LARGE), bytes_accessed=0, transcendentals=0)


def core_kernel(small, arrived, near, far):
    for k in range(2):
        near[k] = small[2 * k] + arrived[2 * k]
        far[k] = small[2 * k + 1] + arrived[2 * k + 1]


def blocks_kernel(arrived, *refs):
    *east, near, far = refs
    for s, block in enumerate(east):
        size = block.shape[0]
        out = (near, far)[s % 2].at[s // 2]
        out[:size, :] = block[...]
        out[size:, :] = arrived[s, : out.shape[0] - size, :]


def far_kernel(near, arrived, own, out):
    own[...] = near[0] + arrived[0]
    out[...] = near[1] + arrived[1]


def add_kernel(small, arrived, out):
    out[...] = small[...] + arrived[...]


def lat_kernel(bit, small, arrived, *refs):
    *before, south, out = refs
    part = jnp.where((lax.axis_index("lat") & bit) != 0, arrived[: south.shape[0], :], 0.0)
    south[...] = before[0][...] + part if before else part
    out[...] = small[...] + arrived[...]


def stream_kernel(east, more, before, small, island, out):
    share, rows, cols = out.shape
    odd = (lax.axis_index("lat") & 1) != 0
    value = east[...] + more[...]
    running = value[: share * rows].reshape(share, rows, cols)
    south = before[...] + jnp.where(odd, value[share * rows :], 0.0)
    row = lax.broadcasted_iota(jnp.int32, (share, rows, cols), 1)
    step = 1
    while step < rows:
        running = running + jnp.where(row >= step, pltpu.roll(running, step, 1), 0.0)
        step *= 2
    circ = small[share:, :]
    label = island[...]
    some = label > 0
    place = jnp.maximum(label - 1, 0)
    for d in range(share):
        g, r = d // 4, d % 4
        constant = jnp.take_along_axis(
            jnp.broadcast_to(circ[r : r + 1, :], (rows, cols)), place + g * NISL, axis=1
        )
        out[d] = running[d] + south[d : d + 1, :] + jnp.where(some, constant, 0.0)


def swap(value, axis, bit):
    n_lat, count = lax.axis_size("lat"), lax.axis_size(axis)
    if axis == "lat":
        return lax.ppermute(value, "lat", [(i, i ^ bit ^ 1) for i in range(n_lat)])
    return lax.ppermute(
        value,
        ("lat", axis),
        [(i * count + j, (i ^ 1) * count + (j ^ bit)) for i in range(n_lat) for j in range(count)],
    )


def shards(thick, zonal, merid, d_zonal, d_merid, d_thick, land_sea, line_label, island_label):
    dirs, levels, rows, cols = d_zonal.shape
    n_lat = lax.axis_size("lat")
    n_lon = lax.axis_size("lon")
    n_dep = lax.axis_size("dep")
    share = dirs // n_dep
    level_scale = 1.0 / math.sqrt(levels * n_dep)
    row_scale = 1.0 / math.sqrt(rows * n_lat)
    line_scale = 1.0 / math.sqrt(rows * n_lat * cols * n_lon / (NISL + 1))
    deep = levels * rows
    base = [x.reshape(deep, cols) for x in (thick, zonal, merid, land_sea)]
    moving = [x.reshape(dirs, deep, cols) for x in (d_zonal, d_merid, d_thick)]
    vmem = pl.BlockSpec(memory_space=pltpu.VMEM)
    hbm = pl.BlockSpec(memory_space=pltpu.HBM)
    params = pltpu.CompilerParams(vmem_limit_bytes=VMEM_BYTES)

    def call(kernel, name, out_shape, *operands, part=0.0):
        return pl.pallas_call(
            kernel,
            out_shape=out_shape,
            in_specs=[vmem] * len(operands),
            out_specs=jax.tree.map(lambda _: vmem, out_shape),
            compiler_params=params,
            cost_estimate=stage(part),
            name=name,
        )(*operands)

    def shape(*sizes):
        return jax.ShapeDtypeStruct(sizes, jnp.float32)

    full = shape(share * rows, cols)
    *east, small, island = pl.pallas_call(
        functools.partial(transport_kernel, -level_scale * row_scale, level_scale * line_scale),
        out_shape=(
            *[full] * n_dep,
            shape(n_dep, share + 8, cols),
            jax.ShapeDtypeStruct((rows, cols), jnp.int32),
        ),
        in_specs=[hbm] * 9,
        out_specs=tuple([vmem] * (n_dep + 2)),
        scratch_shapes=[pltpu.VMEM((deep, cols), jnp.float32)] * 3
        + [pltpu.VMEM((deep, cols), jnp.int32), pltpu.VMEM((rows, cols), jnp.int32)]
        + [pltpu.VMEM((dirs, deep, cols), jnp.bfloat16)] * 3
        + [
            pltpu.VMEM((dirs * rows, cols), jnp.float32),
            pltpu.SemaphoreType.DMA((6,)),
            pltpu.SemaphoreType.DMA((3, n_dep)),
        ],
        compiler_params=params,
        name="transport",
    )(
        *(
            pltpu.with_memory_space_constraint(x, pltpu.HBM)
            for x in (*base, line_label, island_label, *moving)
        )
    )
    arrived = lax.ppermute(small, "lat", [(i, i ^ 1) for i in range(n_lat)])
    two = shape(2, share + 8, cols)
    near, far = call(core_kernel, "core", (two, two), small, arrived, part=PARTS[0])
    full = shape(share * (rows + 1), cols)
    half = shape(share + 8, cols)
    full = shape(share * (rows + 1), cols)
    twice = shape(2, share * (rows + 1), cols)
    large, leaving = call(blocks_kernel, "blocks", (twice, twice), arrived, *east)
    far, leaving = lax.optimization_barrier((far, leaving))
    leaving = lax.ppermute(leaving, "dep", [(i, i ^ 1) for i in range(n_dep)])
    own, out = call(far_kernel, "far", (half, half), near, swap(far, "dep", 1), part=PARTS[1])
    large, leaving = call(far_kernel, "halves", (full, full), large, leaving)
    leaving = lax.ppermute(leaving, "dep", [(i, i ^ 2) for i in range(n_dep)])
    small = call(add_kernel, "near", half, own, swap(out, "dep", 2), part=PARTS[2])
    before = []
    bit = 2
    while bit < n_lat:
        *before, small = call(
            functools.partial(lat_kernel, bit), "bands", (shape(share, cols), half),
            small, swap(small, "lat", bit), *before, part=PARTS[3],
        )
        bit *= 2
    bit = 1
    while 2 * bit < n_lon:
        small = small + swap(small, "lon", bit)
        bit *= 2
    small = call(add_kernel, "lines", half, small, swap(small, "lon", bit), part=PARTS[4])
    return call(
        stream_kernel, "stream", shape(share, rows, cols),
        large, leaving, *before, small, island,
    )


def solution(mesh):
    return jax.shard_map(
        shards,
        mesh=mesh,
        in_specs=(
            P("dep", "lat", "lon"),
            P("dep", "lat", "lon"),
            P("dep", "lat", "lon"),
            P(None, "dep", "lat", "lon"),
            P(None, "dep", "lat", "lon"),
            P(None, "dep", "lat", "lon"),
            P("dep", "lat", "lon"),
            P("lat", "lon"),
            P("lat", "lon"),
        ),
        out_specs=P("dep", "lat", "lon"),
        check_vma=False,
    )
```

```python
import functools
import math

import jax
import jax.numpy as jnp
from jax import lax
from jax.experimental import pallas as pl
from jax.experimental.pallas import tpu as pltpu
from jax.sharding import PartitionSpec as P

NISL = 32
VMEM_BYTES = 16 * 1024 * 1024
LARGE = 700_000_000
PARTS = (0.0, 2.0, 0.8, 0.4, 0.4)


def transport_kernel(
    east_scale, north_scale, thick_hbm, zonal_hbm, merid_hbm, sea_hbm, line_hbm, island_hbm, dz_hbm,
    dm_hbm, dt_hbm, *refs,
):
    (*east, small, island, thick, zonal, merid, sea, line, dz, dm, dt, north, base_sems, sems) = refs
    n_dep = len(east)
    mine = lax.axis_index("dep")
    share = dz.shape[0] // n_dep
    rows, cols = line.shape
    deep = dz.shape[1]
    base = [
        pltpu.make_async_copy(src, dst, base_sems.at[k])
        for k, (src, dst) in enumerate(
            (
                (thick_hbm, thick), (zonal_hbm, zonal), (merid_hbm, merid), (sea_hbm, sea),
                (line_hbm, line), (island_hbm, island),
            )
        )
    ]

    def copies(b):
        part = pl.ds((mine ^ b) * share, share)
        return [
            pltpu.make_async_copy(src.at[part], dst.at[part], sems.at[k, b])
            for k, (src, dst) in enumerate(((dz_hbm, dz), (dm_hbm, dm), (dt_hbm, dt)))
        ]

    for copy in base:
        copy.start()
    for b in reversed(range(n_dep)):
        for copy in copies(b):
            copy.start()
    for copy in base:
        copy.wait()
    wet = sea[...].astype(jnp.float32)
    east_thick = wet * thick[...] * east_scale
    east_base = wet * zonal[...] * east_scale
    north_thick = wet * thick[...] * north_scale
    north_base = wet * merid[...] * north_scale

    def levels(value):
        return jnp.sum(value.reshape(deep // rows, rows, cols), axis=0)

    for b in reversed(range(n_dep)):
        for copy in copies(b):
            copy.wait()
        for d in range(share):
            at = (mine ^ b) * share + d
            z, m, t = (ref[at].astype(jnp.float32) for ref in (dz, dm, dt))
            value = levels(z * east_thick + t * east_base)
            east[b][d * rows : (d + 1) * rows, :] = value
            small[b, d : d + 1, :] = jnp.sum(value, axis=0, keepdims=True)
            at = (b * share + d) * rows
            north[at : at + rows, :] = levels(m * north_thick + t * north_base)
    labels = lax.broadcasted_iota(jnp.int32, (NISL, cols), 0) + 1
    hot = jnp.concatenate(
        [(line[i : i + 1, :] == labels).astype(jnp.bfloat16) for i in range(rows)], axis=1
    )
    dirs = n_dep * share
    value = jnp.concatenate([north[pl.ds(i, dirs, stride=rows), :] for i in range(rows)], axis=1)
    high = value.astype(jnp.bfloat16)
    low = (value - high.astype(jnp.float32)).astype(jnp.bfloat16)
    sums = lax.dot_general(
        jnp.concatenate([high, low], axis=0), hot, (((1,), (1,)), ((), ())),
        preferred_element_type=jnp.float32,
    )
    sums = sums[:dirs] + sums[dirs:]
    quarter = share // 4
    lines = [
        jnp.concatenate(
            [sums[b * share + g * quarter : b * share + (g + 1) * quarter] for g in range(4)],
            axis=1,
        )
        for b in range(n_dep)
    ]
    for b in range(n_dep):
        small[b, share : share + quarter, :] = lines[b]
        small[b, share + quarter :, :] = jnp.zeros((8 - quarter, cols), jnp.float32)


def stage(part):
    return pl.CostEstimate(flops=int(part * LARGE), bytes_accessed=0, transcendentals=0)


def core_kernel(small, arrived, near, far):
    for k in range(2):
        near[k] = small[2 * k] + arrived[2 * k]
        far[k] = small[2 * k + 1] + arrived[2 * k + 1]


def blocks_kernel(arrived, *refs):
    *east, near, far = refs
    for s, block in enumerate(east):
        size = block.shape[0]
        out = (near, far)[s % 2].at[s // 2]
        out[:size, :] = block[...]
        out[size:, :] = arrived[s, : out.shape[0] - size, :]


def far_kernel(near, arrived, own, out):
    own[...] = near[0] + arrived[0]
    out[...] = near[1] + arrived[1]


def add_kernel(small, arrived, out):
    out[...] = small[...] + arrived[...]


def lat_kernel(bit, small, arrived, *refs):
    *before, south, out = refs
    part = jnp.where((lax.axis_index("lat") & bit) != 0, arrived[: south.shape[0], :], 0.0)
    south[...] = before[0][...] + part if before else part
    out[...] = small[...] + arrived[...]


def stream_kernel(east, more, before, small, island, out):
    share, rows, cols = out.shape
    odd = (lax.axis_index("lat") & 1) != 0
    value = east[...] + more[...]
    running = value[: share * rows].reshape(share, rows, cols)
    south = before[...] + jnp.where(odd, value[share * rows :], 0.0)
    row = lax.broadcasted_iota(jnp.int32, (share, rows, cols), 1)
    step = 1
    while step < rows:
        running = running + jnp.where(row >= step, pltpu.roll(running, step, 1), 0.0)
        step *= 2
    circ = small[share:, :]
    label = island[...]
    some = label > 0
    place = jnp.maximum(label - 1, 0)
    for d in range(share):
        g, r = d // 4, d % 4
        constant = jnp.take_along_axis(
            jnp.broadcast_to(circ[r : r + 1, :], (rows, cols)), place + g * NISL, axis=1
        )
        out[d] = running[d] + south[d : d + 1, :] + jnp.where(some, constant, 0.0)


def swap(value, axis, bit):
    n_lat, count = lax.axis_size("lat"), lax.axis_size(axis)
    if axis == "lat":
        return lax.ppermute(value, "lat", [(i, i ^ bit ^ 1) for i in range(n_lat)])
    return lax.ppermute(
        value,
        ("lat", axis),
        [(i * count + j, (i ^ 1) * count + (j ^ bit)) for i in range(n_lat) for j in range(count)],
    )


def shards(thick, zonal, merid, d_zonal, d_merid, d_thick, land_sea, line_label, island_label):
    dirs, levels, rows, cols = d_zonal.shape
    n_lat = lax.axis_size("lat")
    n_lon = lax.axis_size("lon")
    n_dep = lax.axis_size("dep")
    share = dirs // n_dep
    level_scale = 1.0 / math.sqrt(levels * n_dep)
    row_scale = 1.0 / math.sqrt(rows * n_lat)
    line_scale = 1.0 / math.sqrt(rows * n_lat * cols * n_lon / (NISL + 1))
    deep = levels * rows
    base = [x.reshape(deep, cols) for x in (thick, zonal, merid, land_sea)]
    moving = [x.reshape(dirs, deep, cols) for x in (d_zonal, d_merid, d_thick)]
    vmem = pl.BlockSpec(memory_space=pltpu.VMEM)
    hbm = pl.BlockSpec(memory_space=pltpu.HBM)
    params = pltpu.CompilerParams(vmem_limit_bytes=VMEM_BYTES)

    def call(kernel, name, out_shape, *operands, part=0.0):
        return pl.pallas_call(
            kernel,
            out_shape=out_shape,
            in_specs=[vmem] * len(operands),
            out_specs=jax.tree.map(lambda _: vmem, out_shape),
            compiler_params=params,
            cost_estimate=stage(part),
            name=name,
        )(*operands)

    def shape(*sizes):
        return jax.ShapeDtypeStruct(sizes, jnp.float32)

    full = shape(share * rows, cols)
    *east, small, island = pl.pallas_call(
        functools.partial(transport_kernel, -level_scale * row_scale, level_scale * line_scale),
        out_shape=(
            *[full] * n_dep,
            shape(n_dep, share + 8, cols),
            jax.ShapeDtypeStruct((rows, cols), jnp.int32),
        ),
        in_specs=[hbm] * 9,
        out_specs=tuple([vmem] * (n_dep + 2)),
        scratch_shapes=[pltpu.VMEM((deep, cols), jnp.float32)] * 3
        + [pltpu.VMEM((deep, cols), jnp.int32), pltpu.VMEM((rows, cols), jnp.int32)]
        + [pltpu.VMEM((dirs, deep, cols), jnp.bfloat16)] * 3
        + [
            pltpu.VMEM((dirs * rows, cols), jnp.float32),
            pltpu.SemaphoreType.DMA((6,)),
            pltpu.SemaphoreType.DMA((3, n_dep)),
        ],
        compiler_params=params,
        name="transport",
    )(
        *(
            pltpu.with_memory_space_constraint(x, pltpu.HBM)
            for x in (*base, line_label, island_label, *moving)
        )
    )
    arrived = lax.ppermute(small, "lat", [(i, i ^ 1) for i in range(n_lat)])
    two = shape(2, share + 8, cols)
    near, far = call(core_kernel, "core", (two, two), small, arrived, part=PARTS[0])
    full = shape(share * (rows + 1), cols)
    half = shape(share + 8, cols)
    full = shape(share * (rows + 1), cols)
    twice = shape(2, share * (rows + 1), cols)
    large, leaving = call(blocks_kernel, "blocks", (twice, twice), arrived, *east)
    far, leaving = lax.optimization_barrier((far, leaving))
    leaving = lax.ppermute(leaving, "dep", [(i, i ^ 1) for i in range(n_dep)])
    own, out = call(far_kernel, "far", (half, half), near, swap(far, "dep", 1), part=PARTS[1])
    large, leaving = call(far_kernel, "halves", (full, full), large, leaving)
    leaving = lax.ppermute(leaving, "dep", [(i, i ^ 2) for i in range(n_dep)])
    small = call(add_kernel, "near", half, own, swap(out, "dep", 2), part=PARTS[2])
    before = []
    bit = 2
    while bit < n_lat:
        *before, small = call(
            functools.partial(lat_kernel, bit), "bands", (shape(share, cols), half),
            small, swap(small, "lat", bit), *before, part=PARTS[3],
        )
        bit *= 2
    bit = 1
    while 2 * bit < n_lon:
        small = small + swap(small, "lon", bit)
        bit *= 2
    small = call(add_kernel, "lines", half, small, swap(small, "lon", bit), part=PARTS[4])
    return call(
        stream_kernel, "stream", shape(share, rows, cols),
        large, leaving, *before, small, island,
    )


def solution(mesh):
    return jax.shard_map(
        shards,
        mesh=mesh,
        in_specs=(
            P("dep", "lat", "lon"),
            P("dep", "lat", "lon"),
            P("dep", "lat", "lon"),
            P(None, "dep", "lat", "lon"),
            P(None, "dep", "lat", "lon"),
            P(None, "dep", "lat", "lon"),
            P("dep", "lat", "lon"),
            P("lat", "lon"),
            P("lat", "lon"),
        ),
        out_specs=P("dep", "lat", "lon"),
        check_vma=False,
    )
```

```python
import functools
import math

import jax
import jax.numpy as jnp
from jax import lax
from jax.experimental import pallas as pl
from jax.experimental.pallas import tpu as pltpu
from jax.sharding import PartitionSpec as P

NISL = 32
VMEM_BYTES = 16 * 1024 * 1024
LARGE = 700_000_000
PARTS = (0.0, 2.0, 0.8, 0.4, 0.4)


def transport_kernel(
    east_scale, north_scale, thick_hbm, zonal_hbm, merid_hbm, sea_hbm, line_hbm, island_hbm, dz_hbm,
    dm_hbm, dt_hbm, *refs,
):
    (*east, small, island, thick, zonal, merid, sea, line, dz, dm, dt, north, base_sems, sems) = refs
    n_dep = len(east)
    mine = lax.axis_index("dep")
    share = dz.shape[0] // n_dep
    rows, cols = line.shape
    deep = dz.shape[1]
    base = [
        pltpu.make_async_copy(src, dst, base_sems.at[k])
        for k, (src, dst) in enumerate(
            (
                (thick_hbm, thick), (zonal_hbm, zonal), (merid_hbm, merid), (sea_hbm, sea),
                (line_hbm, line), (island_hbm, island),
            )
        )
    ]

    def copies(b):
        part = pl.ds(((mine // 2) ^ b) * 2 * share, 2 * share)
        return [
            pltpu.make_async_copy(src.at[part], dst.at[part], sems.at[k, b])
            for k, (src, dst) in enumerate(((dz_hbm, dz), (dm_hbm, dm), (dt_hbm, dt)))
        ]

    for copy in base:
        copy.start()
    for b in reversed(range(n_dep // 2)):
        for copy in copies(b):
            copy.start()
    for copy in base:
        copy.wait()
    wet = sea[...].astype(jnp.float32)
    east_thick = wet * thick[...] * east_scale
    east_base = wet * zonal[...] * east_scale
    north_thick = wet * thick[...] * north_scale
    north_base = wet * merid[...] * north_scale

    def levels(value):
        return jnp.sum(value.reshape(deep // rows, rows, cols), axis=0)

    for b in reversed(range(n_dep)):
        for copy in copies(b // 2) if b % 2 else ():
            copy.wait()
        for d in range(share):
            at = (mine ^ b) * share + d
            z, m, t = (ref[at].astype(jnp.float32) for ref in (dz, dm, dt))
            value = levels(z * east_thick + t * east_base)
            east[b][d * rows : (d + 1) * rows, :] = value
            small[b, d : d + 1, :] = jnp.sum(value, axis=0, keepdims=True)
            at = (b * share + d) * rows
            north[at : at + rows, :] = levels(m * north_thick + t * north_base)
    labels = lax.broadcasted_iota(jnp.int32, (NISL, cols), 0) + 1
    hot = jnp.concatenate(
        [(line[i : i + 1, :] == labels).astype(jnp.bfloat16) for i in range(rows)], axis=1
    )
    dirs = n_dep * share
    value = jnp.concatenate([north[pl.ds(i, dirs, stride=rows), :] for i in range(rows)], axis=1)
    high = value.astype(jnp.bfloat16)
    low = (value - high.astype(jnp.float32)).astype(jnp.bfloat16)
    sums = lax.dot_general(
        jnp.concatenate([high, low], axis=0), hot, (((1,), (1,)), ((), ())),
        preferred_element_type=jnp.float32,
    )
    sums = sums[:dirs] + sums[dirs:]
    quarter = share // 4
    lines = [
        jnp.concatenate(
            [sums[b * share + g * quarter : b * share + (g + 1) * quarter] for g in range(4)],
            axis=1,
        )
        for b in range(n_dep)
    ]
    for b in range(n_dep):
        small[b, share : share + quarter, :] = lines[b]
        small[b, share + quarter :, :] = jnp.zeros((8 - quarter, cols), jnp.float32)


def stage(part):
    return pl.CostEstimate(flops=int(part * LARGE), bytes_accessed=0, transcendentals=0)


def core_kernel(small, arrived, near, far):
    for k in range(2):
        near[k] = small[2 * k] + arrived[2 * k]
        far[k] = small[2 * k + 1] + arrived[2 * k + 1]


def blocks_kernel(arrived, *refs):
    *east, near, far = refs
    for s, block in enumerate(east):
        size = block.shape[0]
        out = (near, far)[s % 2].at[s // 2]
        out[:size, :] = block[...]
        out[size:, :] = arrived[s, : out.shape[0] - size, :]


def far_kernel(near, arrived, own, out):
    own[...] = near[0] + arrived[0]
    out[...] = near[1] + arrived[1]


def add_kernel(small, arrived, out):
    out[...] = small[...] + arrived[...]


def lat_kernel(bit, small, arrived, *refs):
    *before, south, out = refs
    part = jnp.where((lax.axis_index("lat") & bit) != 0, arrived[: south.shape[0], :], 0.0)
    south[...] = before[0][...] + part if before else part
    out[...] = small[...] + arrived[...]


def stream_kernel(east, more, before, small, island, out):
    share, rows, cols = out.shape
    odd = (lax.axis_index("lat") & 1) != 0
    value = east[...] + more[...]
    running = value[: share * rows].reshape(share, rows, cols)
    south = before[...] + jnp.where(odd, value[share * rows :], 0.0)
    row = lax.broadcasted_iota(jnp.int32, (share, rows, cols), 1)
    step = 1
    while step < rows:
        running = running + jnp.where(row >= step, pltpu.roll(running, step, 1), 0.0)
        step *= 2
    circ = small[share:, :]
    label = island[...]
    some = label > 0
    place = jnp.maximum(label - 1, 0)
    for d in range(share):
        g, r = d // 4, d % 4
        constant = jnp.take_along_axis(
            jnp.broadcast_to(circ[r : r + 1, :], (rows, cols)), place + g * NISL, axis=1
        )
        out[d] = running[d] + south[d : d + 1, :] + jnp.where(some, constant, 0.0)


def swap(value, axis, bit):
    n_lat, count = lax.axis_size("lat"), lax.axis_size(axis)
    if axis == "lat":
        return lax.ppermute(value, "lat", [(i, i ^ bit ^ 1) for i in range(n_lat)])
    return lax.ppermute(
        value,
        ("lat", axis),
        [(i * count + j, (i ^ 1) * count + (j ^ bit)) for i in range(n_lat) for j in range(count)],
    )


def shards(thick, zonal, merid, d_zonal, d_merid, d_thick, land_sea, line_label, island_label):
    dirs, levels, rows, cols = d_zonal.shape
    n_lat = lax.axis_size("lat")
    n_lon = lax.axis_size("lon")
    n_dep = lax.axis_size("dep")
    share = dirs // n_dep
    level_scale = 1.0 / math.sqrt(levels * n_dep)
    row_scale = 1.0 / math.sqrt(rows * n_lat)
    line_scale = 1.0 / math.sqrt(rows * n_lat * cols * n_lon / (NISL + 1))
    deep = levels * rows
    base = [x.reshape(deep, cols) for x in (thick, zonal, merid, land_sea)]
    moving = [x.reshape(dirs, deep, cols) for x in (d_zonal, d_merid, d_thick)]
    vmem = pl.BlockSpec(memory_space=pltpu.VMEM)
    hbm = pl.BlockSpec(memory_space=pltpu.HBM)
    params = pltpu.CompilerParams(vmem_limit_bytes=VMEM_BYTES)

    def call(kernel, name, out_shape, *operands, part=0.0):
        return pl.pallas_call(
            kernel,
            out_shape=out_shape,
            in_specs=[vmem] * len(operands),
            out_specs=jax.tree.map(lambda _: vmem, out_shape),
            compiler_params=params,
            cost_estimate=stage(part),
            name=name,
        )(*operands)

    def shape(*sizes):
        return jax.ShapeDtypeStruct(sizes, jnp.float32)

    full = shape(share * rows, cols)
    *east, small, island = pl.pallas_call(
        functools.partial(transport_kernel, -level_scale * row_scale, level_scale * line_scale),
        out_shape=(
            *[full] * n_dep,
            shape(n_dep, share + 8, cols),
            jax.ShapeDtypeStruct((rows, cols), jnp.int32),
        ),
        in_specs=[hbm] * 9,
        out_specs=tuple([vmem] * (n_dep + 2)),
        scratch_shapes=[pltpu.VMEM((deep, cols), jnp.float32)] * 3
        + [pltpu.VMEM((deep, cols), jnp.int32), pltpu.VMEM((rows, cols), jnp.int32)]
        + [pltpu.VMEM((dirs, deep, cols), jnp.bfloat16)] * 3
        + [
            pltpu.VMEM((dirs * rows, cols), jnp.float32),
            pltpu.SemaphoreType.DMA((6,)),
            pltpu.SemaphoreType.DMA((3, n_dep // 2)),
        ],
        compiler_params=params,
        name="transport",
    )(
        *(
            pltpu.with_memory_space_constraint(x, pltpu.HBM)
            for x in (*base, line_label, island_label, *moving)
        )
    )
    arrived = lax.ppermute(small, "lat", [(i, i ^ 1) for i in range(n_lat)])
    two = shape(2, share + 8, cols)
    near, far = call(core_kernel, "core", (two, two), small, arrived, part=PARTS[0])
    full = shape(share * (rows + 1), cols)
    half = shape(share + 8, cols)
    full = shape(share * (rows + 1), cols)
    twice = shape(2, share * (rows + 1), cols)
    large, leaving = call(blocks_kernel, "blocks", (twice, twice), arrived, *east)
    far, leaving = lax.optimization_barrier((far, leaving))
    leaving = lax.ppermute(leaving, "dep", [(i, i ^ 1) for i in range(n_dep)])
    own, out = call(far_kernel, "far", (half, half), near, swap(far, "dep", 1), part=PARTS[1])
    large, leaving = call(far_kernel, "halves", (full, full), large, leaving)
    leaving = lax.ppermute(leaving, "dep", [(i, i ^ 2) for i in range(n_dep)])
    small = call(add_kernel, "near", half, own, swap(out, "dep", 2), part=PARTS[2])
    before = []
    bit = 2
    while bit < n_lat:
        *before, small = call(
            functools.partial(lat_kernel, bit), "bands", (shape(share, cols), half),
            small, swap(small, "lat", bit), *before, part=PARTS[3],
        )
        bit *= 2
    bit = 1
    while 2 * bit < n_lon:
        small = small + swap(small, "lon", bit)
        bit *= 2
    small = call(add_kernel, "lines", half, small, swap(small, "lon", bit), part=PARTS[4])
    return call(
        stream_kernel, "stream", shape(share, rows, cols),
        large, leaving, *before, small, island,
    )


def solution(mesh):
    return jax.shard_map(
        shards,
        mesh=mesh,
        in_specs=(
            P("dep", "lat", "lon"),
            P("dep", "lat", "lon"),
            P("dep", "lat", "lon"),
            P(None, "dep", "lat", "lon"),
            P(None, "dep", "lat", "lon"),
            P(None, "dep", "lat", "lon"),
            P("dep", "lat", "lon"),
            P("lat", "lon"),
            P("lat", "lon"),
        ),
        out_specs=P("dep", "lat", "lon"),
        check_vma=False,
    )
```

```python
import functools
import math

import jax
import jax.numpy as jnp
from jax import lax
from jax.experimental import pallas as pl
from jax.experimental.pallas import tpu as pltpu
from jax.sharding import PartitionSpec as P

NISL = 32
VMEM_BYTES = 16 * 1024 * 1024
LARGE = 700_000_000
PARTS = (0.0, 2.0, 0.8, 0.4, 0.4)


def transport_kernel(
    east_scale, north_scale, thick_hbm, zonal_hbm, merid_hbm, sea_hbm, line_hbm, island_hbm, dz_hbm,
    dm_hbm, dt_hbm, *refs,
):
    (*east, small, island, thick, zonal, merid, sea, line, dz, dm, dt, north, base_sems, sems) = refs
    n_dep = len(east)
    mine = lax.axis_index("dep")
    share = dz.shape[0] // n_dep
    rows, cols = line.shape
    deep = dz.shape[1]
    base = [
        pltpu.make_async_copy(src, dst, base_sems.at[k])
        for k, (src, dst) in enumerate(
            (
                (thick_hbm, thick), (zonal_hbm, zonal), (merid_hbm, merid), (sea_hbm, sea),
                (line_hbm, line), (island_hbm, island),
            )
        )
    ]

    copies = [
        pltpu.make_async_copy(src, dst, sems.at[k])
        for k, (src, dst) in enumerate(((dz_hbm, dz), (dm_hbm, dm), (dt_hbm, dt)))
    ]

    for copy in base:
        copy.start()
    for copy in copies:
        copy.start()
    for copy in base:
        copy.wait()
    wet = sea[...].astype(jnp.float32)
    east_thick = wet * thick[...] * east_scale
    east_base = wet * zonal[...] * east_scale
    north_thick = wet * thick[...] * north_scale
    north_base = wet * merid[...] * north_scale

    def levels(value):
        return jnp.sum(value.reshape(deep // rows, rows, cols), axis=0)

    for copy in copies:
        copy.wait()
    for b in reversed(range(n_dep)):
        for d in range(share):
            at = (mine ^ b) * share + d
            z, m, t = (ref[at].astype(jnp.float32) for ref in (dz, dm, dt))
            value = levels(z * east_thick + t * east_base)
            east[b][d * rows : (d + 1) * rows, :] = value
            small[b, d : d + 1, :] = jnp.sum(value, axis=0, keepdims=True)
            at = (b * share + d) * rows
            north[at : at + rows, :] = levels(m * north_thick + t * north_base)
    labels = lax.broadcasted_iota(jnp.int32, (NISL, cols), 0) + 1
    hot = jnp.concatenate(
        [(line[i : i + 1, :] == labels).astype(jnp.bfloat16) for i in range(rows)], axis=1
    )
    dirs = n_dep * share
    value = jnp.concatenate([north[pl.ds(i, dirs, stride=rows), :] for i in range(rows)], axis=1)
    high = value.astype(jnp.bfloat16)
    low = (value - high.astype(jnp.float32)).astype(jnp.bfloat16)
    sums = lax.dot_general(
        jnp.concatenate([high, low], axis=0), hot, (((1,), (1,)), ((), ())),
        preferred_element_type=jnp.float32,
    )
    sums = sums[:dirs] + sums[dirs:]
    quarter = share // 4
    lines = [
        jnp.concatenate(
            [sums[b * share + g * quarter : b * share + (g + 1) * quarter] for g in range(4)],
            axis=1,
        )
        for b in range(n_dep)
    ]
    for b in range(n_dep):
        small[b, share : share + quarter, :] = lines[b]
        small[b, share + quarter :, :] = jnp.zeros((8 - quarter, cols), jnp.float32)


def stage(part):
    return pl.CostEstimate(flops=int(part * LARGE), bytes_accessed=0, transcendentals=0)


def core_kernel(small, arrived, near, far):
    for k in range(2):
        near[k] = small[2 * k] + arrived[2 * k]
        far[k] = small[2 * k + 1] + arrived[2 * k + 1]


def blocks_kernel(arrived, *refs):
    *east, near, far = refs
    for s, block in enumerate(east):
        size = block.shape[0]
        out = (near, far)[s % 2].at[s // 2]
        out[:size, :] = block[...]
        out[size:, :] = arrived[s, : out.shape[0] - size, :]


def far_kernel(near, arrived, own, out):
    own[...] = near[0] + arrived[0]
    out[...] = near[1] + arrived[1]


def add_kernel(small, arrived, out):
    out[...] = small[...] + arrived[...]


def lat_kernel(bit, small, arrived, *refs):
    *before, south, out = refs
    part = jnp.where((lax.axis_index("lat") & bit) != 0, arrived[: south.shape[0], :], 0.0)
    south[...] = before[0][...] + part if before else part
    out[...] = small[...] + arrived[...]


def stream_kernel(east, more, before, small, island, out):
    share, rows, cols = out.shape
    odd = (lax.axis_index("lat") & 1) != 0
    value = east[...] + more[...]
    running = value[: share * rows].reshape(share, rows, cols)
    south = before[...] + jnp.where(odd, value[share * rows :], 0.0)
    row = lax.broadcasted_iota(jnp.int32, (share, rows, cols), 1)
    step = 1
    while step < rows:
        running = running + jnp.where(row >= step, pltpu.roll(running, step, 1), 0.0)
        step *= 2
    circ = small[share:, :]
    label = island[...]
    some = label > 0
    place = jnp.maximum(label - 1, 0)
    for d in range(share):
        g, r = d // 4, d % 4
        constant = jnp.take_along_axis(
            jnp.broadcast_to(circ[r : r + 1, :], (rows, cols)), place + g * NISL, axis=1
        )
        out[d] = running[d] + south[d : d + 1, :] + jnp.where(some, constant, 0.0)


def swap(value, axis, bit):
    n_lat, count = lax.axis_size("lat"), lax.axis_size(axis)
    if axis == "lat":
        return lax.ppermute(value, "lat", [(i, i ^ bit ^ 1) for i in range(n_lat)])
    return lax.ppermute(
        value,
        ("lat", axis),
        [(i * count + j, (i ^ 1) * count + (j ^ bit)) for i in range(n_lat) for j in range(count)],
    )


def shards(thick, zonal, merid, d_zonal, d_merid, d_thick, land_sea, line_label, island_label):
    dirs, levels, rows, cols = d_zonal.shape
    n_lat = lax.axis_size("lat")
    n_lon = lax.axis_size("lon")
    n_dep = lax.axis_size("dep")
    share = dirs // n_dep
    level_scale = 1.0 / math.sqrt(levels * n_dep)
    row_scale = 1.0 / math.sqrt(rows * n_lat)
    line_scale = 1.0 / math.sqrt(rows * n_lat * cols * n_lon / (NISL + 1))
    deep = levels * rows
    base = [x.reshape(deep, cols) for x in (thick, zonal, merid, land_sea)]
    moving = [x.reshape(dirs, deep, cols) for x in (d_zonal, d_merid, d_thick)]
    vmem = pl.BlockSpec(memory_space=pltpu.VMEM)
    hbm = pl.BlockSpec(memory_space=pltpu.HBM)
    params = pltpu.CompilerParams(vmem_limit_bytes=VMEM_BYTES)

    def call(kernel, name, out_shape, *operands, part=0.0):
        return pl.pallas_call(
            kernel,
            out_shape=out_shape,
            in_specs=[vmem] * len(operands),
            out_specs=jax.tree.map(lambda _: vmem, out_shape),
            compiler_params=params,
            cost_estimate=stage(part),
            name=name,
        )(*operands)

    def shape(*sizes):
        return jax.ShapeDtypeStruct(sizes, jnp.float32)

    full = shape(share * rows, cols)
    *east, small, island = pl.pallas_call(
        functools.partial(transport_kernel, -level_scale * row_scale, level_scale * line_scale),
        out_shape=(
            *[full] * n_dep,
            shape(n_dep, share + 8, cols),
            jax.ShapeDtypeStruct((rows, cols), jnp.int32),
        ),
        in_specs=[hbm] * 9,
        out_specs=tuple([vmem] * (n_dep + 2)),
        scratch_shapes=[pltpu.VMEM((deep, cols), jnp.float32)] * 3
        + [pltpu.VMEM((deep, cols), jnp.int32), pltpu.VMEM((rows, cols), jnp.int32)]
        + [pltpu.VMEM((dirs, deep, cols), jnp.bfloat16)] * 3
        + [
            pltpu.VMEM((dirs * rows, cols), jnp.float32),
            pltpu.SemaphoreType.DMA((6,)),
            pltpu.SemaphoreType.DMA((3,)),
        ],
        compiler_params=params,
        name="transport",
    )(
        *(
            pltpu.with_memory_space_constraint(x, pltpu.HBM)
            for x in (*base, line_label, island_label, *moving)
        )
    )
    arrived = lax.ppermute(small, "lat", [(i, i ^ 1) for i in range(n_lat)])
    two = shape(2, share + 8, cols)
    near, far = call(core_kernel, "core", (two, two), small, arrived, part=PARTS[0])
    full = shape(share * (rows + 1), cols)
    half = shape(share + 8, cols)
    full = shape(share * (rows + 1), cols)
    twice = shape(2, share * (rows + 1), cols)
    large, leaving = call(blocks_kernel, "blocks", (twice, twice), arrived, *east)
    far, leaving = lax.optimization_barrier((far, leaving))
    leaving = lax.ppermute(leaving, "dep", [(i, i ^ 1) for i in range(n_dep)])
    own, out = call(far_kernel, "far", (half, half), near, swap(far, "dep", 1), part=PARTS[1])
    large, leaving = call(far_kernel, "halves", (full, full), large, leaving)
    leaving = lax.ppermute(leaving, "dep", [(i, i ^ 2) for i in range(n_dep)])
    small = call(add_kernel, "near", half, own, swap(out, "dep", 2), part=PARTS[2])
    before = []
    bit = 2
    while bit < n_lat:
        *before, small = call(
            functools.partial(lat_kernel, bit), "bands", (shape(share, cols), half),
            small, swap(small, "lat", bit), *before, part=PARTS[3],
        )
        bit *= 2
    bit = 1
    while 2 * bit < n_lon:
        small = small + swap(small, "lon", bit)
        bit *= 2
    small = call(add_kernel, "lines", half, small, swap(small, "lon", bit), part=PARTS[4])
    return call(
        stream_kernel, "stream", shape(share, rows, cols),
        large, leaving, *before, small, island,
    )


def solution(mesh):
    return jax.shard_map(
        shards,
        mesh=mesh,
        in_specs=(
            P("dep", "lat", "lon"),
            P("dep", "lat", "lon"),
            P("dep", "lat", "lon"),
            P(None, "dep", "lat", "lon"),
            P(None, "dep", "lat", "lon"),
            P(None, "dep", "lat", "lon"),
            P("dep", "lat", "lon"),
            P("lat", "lon"),
            P("lat", "lon"),
        ),
        out_specs=P("dep", "lat", "lon"),
        check_vma=False,
    )
```

```python
import functools
import math

import jax
import jax.numpy as jnp
from jax import lax
from jax.experimental import pallas as pl
from jax.experimental.pallas import tpu as pltpu
from jax.sharding import PartitionSpec as P

NISL = 32
VMEM_BYTES = 16 * 1024 * 1024
LARGE = 700_000_000
PARTS = (0.0, 2.0, 0.8, 0.4, 0.4)


def transport_kernel(
    east_scale, north_scale, thick_hbm, zonal_hbm, merid_hbm, sea_hbm, line_hbm, island_hbm, dz_hbm,
    dm_hbm, dt_hbm, *refs,
):
    (*east, small, island, thick, zonal, merid, sea, line, dz, dm, dt, north, base_sems, sems) = refs
    n_dep = len(east)
    mine = lax.axis_index("dep")
    share = dz.shape[0] // n_dep
    rows, cols = line.shape
    deep = dz.shape[1]
    base = [
        pltpu.make_async_copy(src, dst, base_sems.at[k])
        for k, (src, dst) in enumerate(
            (
                (thick_hbm, thick), (zonal_hbm, zonal), (merid_hbm, merid), (sea_hbm, sea),
                (line_hbm, line), (island_hbm, island),
            )
        )
    ]

    def copies(b):
        part = pl.ds(((mine // 2) ^ b) * 2 * share, 2 * share)
        return [
            pltpu.make_async_copy(src.at[part], dst.at[part], sems.at[k, b])
            for k, (src, dst) in enumerate(((dz_hbm, dz), (dm_hbm, dm), (dt_hbm, dt)))
        ]

    for b in reversed(range(n_dep // 2)):
        for copy in copies(b):
            copy.start()
        for copy in base if b == n_dep // 2 - 1 else ():
            copy.start()
    for copy in base:
        copy.wait()
    wet = sea[...].astype(jnp.float32)
    east_thick = wet * thick[...] * east_scale
    east_base = wet * zonal[...] * east_scale
    north_thick = wet * thick[...] * north_scale
    north_base = wet * merid[...] * north_scale

    def levels(value):
        return jnp.sum(value.reshape(deep // rows, rows, cols), axis=0)

    for b in reversed(range(n_dep)):
        for copy in copies(b // 2) if b % 2 else ():
            copy.wait()
        for d in range(share):
            at = (mine ^ b) * share + d
            z, m, t = (ref[at].astype(jnp.float32) for ref in (dz, dm, dt))
            value = levels(z * east_thick + t * east_base)
            east[b][d * rows : (d + 1) * rows, :] = value
            small[b, d : d + 1, :] = jnp.sum(value, axis=0, keepdims=True)
            at = (b * share + d) * rows
            north[at : at + rows, :] = levels(m * north_thick + t * north_base)
    labels = lax.broadcasted_iota(jnp.int32, (NISL, cols), 0) + 1
    hot = jnp.concatenate(
        [(line[i : i + 1, :] == labels).astype(jnp.bfloat16) for i in range(rows)], axis=1
    )
    dirs = n_dep * share
    value = jnp.concatenate([north[pl.ds(i, dirs, stride=rows), :] for i in range(rows)], axis=1)
    high = value.astype(jnp.bfloat16)
    low = (value - high.astype(jnp.float32)).astype(jnp.bfloat16)
    sums = lax.dot_general(
        jnp.concatenate([high, low], axis=0), hot, (((1,), (1,)), ((), ())),
        preferred_element_type=jnp.float32,
    )
    sums = sums[:dirs] + sums[dirs:]
    quarter = share // 4
    lines = [
        jnp.concatenate(
            [sums[b * share + g * quarter : b * share + (g + 1) * quarter] for g in range(4)],
            axis=1,
        )
        for b in range(n_dep)
    ]
    for b in range(n_dep):
        small[b, share : share + quarter, :] = lines[b]
        small[b, share + quarter :, :] = jnp.zeros((8 - quarter, cols), jnp.float32)


def stage(part):
    return pl.CostEstimate(flops=int(part * LARGE), bytes_accessed=0, transcendentals=0)


def core_kernel(small, arrived, near, far):
    for k in range(2):
        near[k] = small[2 * k] + arrived[2 * k]
        far[k] = small[2 * k + 1] + arrived[2 * k + 1]


def blocks_kernel(arrived, *refs):
    *east, near, far = refs
    for s, block in enumerate(east):
        size = block.shape[0]
        out = (near, far)[s % 2].at[s // 2]
        out[:size, :] = block[...]
        out[size:, :] = arrived[s, : out.shape[0] - size, :]


def far_kernel(near, arrived, own, out):
    own[...] = near[0] + arrived[0]
    out[...] = near[1] + arrived[1]


def add_kernel(small, arrived, out):
    out[...] = small[...] + arrived[...]


def lat_kernel(bit, small, arrived, *refs):
    *before, south, out = refs
    part = jnp.where((lax.axis_index("lat") & bit) != 0, arrived[: south.shape[0], :], 0.0)
    south[...] = before[0][...] + part if before else part
    out[...] = small[...] + arrived[...]


def stream_kernel(east, more, before, small, island, out):
    share, rows, cols = out.shape
    odd = (lax.axis_index("lat") & 1) != 0
    value = east[...] + more[...]
    running = value[: share * rows].reshape(share, rows, cols)
    south = before[...] + jnp.where(odd, value[share * rows :], 0.0)
    row = lax.broadcasted_iota(jnp.int32, (share, rows, cols), 1)
    step = 1
    while step < rows:
        running = running + jnp.where(row >= step, pltpu.roll(running, step, 1), 0.0)
        step *= 2
    circ = small[share:, :]
    label = island[...]
    some = label > 0
    place = jnp.maximum(label - 1, 0)
    for d in range(share):
        g, r = d // 4, d % 4
        constant = jnp.take_along_axis(
            jnp.broadcast_to(circ[r : r + 1, :], (rows, cols)), place + g * NISL, axis=1
        )
        out[d] = running[d] + south[d : d + 1, :] + jnp.where(some, constant, 0.0)


def swap(value, axis, bit):
    n_lat, count = lax.axis_size("lat"), lax.axis_size(axis)
    if axis == "lat":
        return lax.ppermute(value, "lat", [(i, i ^ bit ^ 1) for i in range(n_lat)])
    return lax.ppermute(
        value,
        ("lat", axis),
        [(i * count + j, (i ^ 1) * count + (j ^ bit)) for i in range(n_lat) for j in range(count)],
    )


def shards(thick, zonal, merid, d_zonal, d_merid, d_thick, land_sea, line_label, island_label):
    dirs, levels, rows, cols = d_zonal.shape
    n_lat = lax.axis_size("lat")
    n_lon = lax.axis_size("lon")
    n_dep = lax.axis_size("dep")
    share = dirs // n_dep
    level_scale = 1.0 / math.sqrt(levels * n_dep)
    row_scale = 1.0 / math.sqrt(rows * n_lat)
    line_scale = 1.0 / math.sqrt(rows * n_lat * cols * n_lon / (NISL + 1))
    deep = levels * rows
    base = [x.reshape(deep, cols) for x in (thick, zonal, merid, land_sea)]
    moving = [x.reshape(dirs, deep, cols) for x in (d_zonal, d_merid, d_thick)]
    vmem = pl.BlockSpec(memory_space=pltpu.VMEM)
    hbm = pl.BlockSpec(memory_space=pltpu.HBM)
    params = pltpu.CompilerParams(vmem_limit_bytes=VMEM_BYTES)

    def call(kernel, name, out_shape, *operands, part=0.0):
        return pl.pallas_call(
            kernel,
            out_shape=out_shape,
            in_specs=[vmem] * len(operands),
            out_specs=jax.tree.map(lambda _: vmem, out_shape),
            compiler_params=params,
            cost_estimate=stage(part),
            name=name,
        )(*operands)

    def shape(*sizes):
        return jax.ShapeDtypeStruct(sizes, jnp.float32)

    full = shape(share * rows, cols)
    *east, small, island = pl.pallas_call(
        functools.partial(transport_kernel, -level_scale * row_scale, level_scale * line_scale),
        out_shape=(
            *[full] * n_dep,
            shape(n_dep, share + 8, cols),
            jax.ShapeDtypeStruct((rows, cols), jnp.int32),
        ),
        in_specs=[hbm] * 9,
        out_specs=tuple([vmem] * (n_dep + 2)),
        scratch_shapes=[pltpu.VMEM((deep, cols), jnp.float32)] * 3
        + [pltpu.VMEM((deep, cols), jnp.int32), pltpu.VMEM((rows, cols), jnp.int32)]
        + [pltpu.VMEM((dirs, deep, cols), jnp.bfloat16)] * 3
        + [
            pltpu.VMEM((dirs * rows, cols), jnp.float32),
            pltpu.SemaphoreType.DMA((6,)),
            pltpu.SemaphoreType.DMA((3, n_dep // 2)),
        ],
        compiler_params=params,
        name="transport",
    )(
        *(
            pltpu.with_memory_space_constraint(x, pltpu.HBM)
            for x in (*base, line_label, island_label, *moving)
        )
    )
    arrived = lax.ppermute(small, "lat", [(i, i ^ 1) for i in range(n_lat)])
    two = shape(2, share + 8, cols)
    near, far = call(core_kernel, "core", (two, two), small, arrived, part=PARTS[0])
    full = shape(share * (rows + 1), cols)
    half = shape(share + 8, cols)
    full = shape(share * (rows + 1), cols)
    twice = shape(2, share * (rows + 1), cols)
    large, leaving = call(blocks_kernel, "blocks", (twice, twice), arrived, *east)
    far, leaving = lax.optimization_barrier((far, leaving))
    leaving = lax.ppermute(leaving, "dep", [(i, i ^ 1) for i in range(n_dep)])
    own, out = call(far_kernel, "far", (half, half), near, swap(far, "dep", 1), part=PARTS[1])
    large, leaving = call(far_kernel, "halves", (full, full), large, leaving)
    leaving = lax.ppermute(leaving, "dep", [(i, i ^ 2) for i in range(n_dep)])
    small = call(add_kernel, "near", half, own, swap(out, "dep", 2), part=PARTS[2])
    before = []
    bit = 2
    while bit < n_lat:
        *before, small = call(
            functools.partial(lat_kernel, bit), "bands", (shape(share, cols), half),
            small, swap(small, "lat", bit), *before, part=PARTS[3],
        )
        bit *= 2
    bit = 1
    while 2 * bit < n_lon:
        small = small + swap(small, "lon", bit)
        bit *= 2
    small = call(add_kernel, "lines", half, small, swap(small, "lon", bit), part=PARTS[4])
    return call(
        stream_kernel, "stream", shape(share, rows, cols),
        large, leaving, *before, small, island,
    )


def solution(mesh):
    return jax.shard_map(
        shards,
        mesh=mesh,
        in_specs=(
            P("dep", "lat", "lon"),
            P("dep", "lat", "lon"),
            P("dep", "lat", "lon"),
            P(None, "dep", "lat", "lon"),
            P(None, "dep", "lat", "lon"),
            P(None, "dep", "lat", "lon"),
            P("dep", "lat", "lon"),
            P("lat", "lon"),
            P("lat", "lon"),
        ),
        out_specs=P("dep", "lat", "lon"),
        check_vma=False,
    )
```

```python
import functools
import math

import jax
import jax.numpy as jnp
from jax import lax
from jax.experimental import pallas as pl
from jax.experimental.pallas import tpu as pltpu
from jax.sharding import PartitionSpec as P

NISL = 32
VMEM_BYTES = 16 * 1024 * 1024
LARGE = 700_000_000
PARTS = (0.0, 2.0, 0.8, 0.4, 0.4)


def transport_kernel(
    east_scale, north_scale, thick_hbm, zonal_hbm, merid_hbm, sea_hbm, line_hbm, island_hbm, dz_hbm,
    dm_hbm, dt_hbm, *refs,
):
    (*east, small, island, thick, zonal, merid, sea, line, dz, dm, dt, north, base_sems, sems) = refs
    n_dep = len(east)
    mine = lax.axis_index("dep")
    share = dz.shape[0] // n_dep
    rows, cols = line.shape
    deep = dz.shape[1]
    base = [
        pltpu.make_async_copy(src, dst, base_sems.at[k])
        for k, (src, dst) in enumerate(
            (
                (thick_hbm, thick), (zonal_hbm, zonal), (merid_hbm, merid), (sea_hbm, sea),
                (line_hbm, line), (island_hbm, island),
            )
        )
    ]

    def copies(b):
        part = pl.ds(((mine // 2) ^ b) * 2 * share, 2 * share)
        return [
            pltpu.make_async_copy(src.at[part], dst.at[part], sems.at[k, b])
            for k, (src, dst) in enumerate(((dz_hbm, dz), (dm_hbm, dm), (dt_hbm, dt)))
        ]

    for copy in base:
        copy.start()
    for b in reversed(range(n_dep // 2)):
        for copy in copies(b):
            copy.start()
    for copy in base:
        copy.wait()
    wet = sea[...].astype(jnp.float32)
    east_thick = wet * thick[...] * east_scale
    east_base = wet * zonal[...] * east_scale
    north_thick = wet * thick[...] * north_scale
    north_base = wet * merid[...] * north_scale

    def levels(value):
        return jnp.sum(value.reshape(deep // rows, rows, cols), axis=0)

    for b in reversed(range(n_dep)):
        if b == 1:
            labels = lax.broadcasted_iota(jnp.int32, (NISL, cols), 0) + 1
            hot = jnp.concatenate(
                [(line[i : i + 1, :] == labels).astype(jnp.bfloat16) for i in range(rows)], axis=1
            )
        for copy in copies(b // 2) if b % 2 else ():
            copy.wait()
        for d in range(share):
            at = (mine ^ b) * share + d
            z, m, t = (ref[at].astype(jnp.float32) for ref in (dz, dm, dt))
            value = levels(z * east_thick + t * east_base)
            east[b][d * rows : (d + 1) * rows, :] = value
            small[b, d : d + 1, :] = jnp.sum(value, axis=0, keepdims=True)
            at = (b * share + d) * rows
            north[at : at + rows, :] = levels(m * north_thick + t * north_base)
    dirs = n_dep * share
    value = jnp.concatenate([north[pl.ds(i, dirs, stride=rows), :] for i in range(rows)], axis=1)
    high = value.astype(jnp.bfloat16)
    low = (value - high.astype(jnp.float32)).astype(jnp.bfloat16)
    sums = lax.dot_general(
        jnp.concatenate([high, low], axis=0), hot, (((1,), (1,)), ((), ())),
        preferred_element_type=jnp.float32,
    )
    sums = sums[:dirs] + sums[dirs:]
    quarter = share // 4
    lines = [
        jnp.concatenate(
            [sums[b * share + g * quarter : b * share + (g + 1) * quarter] for g in range(4)],
            axis=1,
        )
        for b in range(n_dep)
    ]
    for b in range(n_dep):
        small[b, share : share + quarter, :] = lines[b]
        small[b, share + quarter :, :] = jnp.zeros((8 - quarter, cols), jnp.float32)


def stage(part):
    return pl.CostEstimate(flops=int(part * LARGE), bytes_accessed=0, transcendentals=0)


def core_kernel(small, arrived, near, far):
    for k in range(2):
        near[k] = small[2 * k] + arrived[2 * k]
        far[k] = small[2 * k + 1] + arrived[2 * k + 1]


def blocks_kernel(arrived, *refs):
    *east, near, far = refs
    for s, block in enumerate(east):
        size = block.shape[0]
        out = (near, far)[s % 2].at[s // 2]
        out[:size, :] = block[...]
        out[size:, :] = arrived[s, : out.shape[0] - size, :]


def far_kernel(near, arrived, own, out):
    own[...] = near[0] + arrived[0]
    out[...] = near[1] + arrived[1]


def add_kernel(small, arrived, out):
    out[...] = small[...] + arrived[...]


def lat_kernel(bit, small, arrived, *refs):
    *before, south, out = refs
    part = jnp.where((lax.axis_index("lat") & bit) != 0, arrived[: south.shape[0], :], 0.0)
    south[...] = before[0][...] + part if before else part
    out[...] = small[...] + arrived[...]


def stream_kernel(east, more, before, small, island, out):
    share, rows, cols = out.shape
    odd = (lax.axis_index("lat") & 1) != 0
    value = east[...] + more[...]
    running = value[: share * rows].reshape(share, rows, cols)
    south = before[...] + jnp.where(odd, value[share * rows :], 0.0)
    row = lax.broadcasted_iota(jnp.int32, (share, rows, cols), 1)
    step = 1
    while step < rows:
        running = running + jnp.where(row >= step, pltpu.roll(running, step, 1), 0.0)
        step *= 2
    circ = small[share:, :]
    label = island[...]
    some = label > 0
    place = jnp.maximum(label - 1, 0)
    for d in range(share):
        g, r = d // 4, d % 4
        constant = jnp.take_along_axis(
            jnp.broadcast_to(circ[r : r + 1, :], (rows, cols)), place + g * NISL, axis=1
        )
        out[d] = running[d] + south[d : d + 1, :] + jnp.where(some, constant, 0.0)


def swap(value, axis, bit):
    n_lat, count = lax.axis_size("lat"), lax.axis_size(axis)
    if axis == "lat":
        return lax.ppermute(value, "lat", [(i, i ^ bit ^ 1) for i in range(n_lat)])
    return lax.ppermute(
        value,
        ("lat", axis),
        [(i * count + j, (i ^ 1) * count + (j ^ bit)) for i in range(n_lat) for j in range(count)],
    )


def shards(thick, zonal, merid, d_zonal, d_merid, d_thick, land_sea, line_label, island_label):
    dirs, levels, rows, cols = d_zonal.shape
    n_lat = lax.axis_size("lat")
    n_lon = lax.axis_size("lon")
    n_dep = lax.axis_size("dep")
    share = dirs // n_dep
    level_scale = 1.0 / math.sqrt(levels * n_dep)
    row_scale = 1.0 / math.sqrt(rows * n_lat)
    line_scale = 1.0 / math.sqrt(rows * n_lat * cols * n_lon / (NISL + 1))
    deep = levels * rows
    base = [x.reshape(deep, cols) for x in (thick, zonal, merid, land_sea)]
    moving = [x.reshape(dirs, deep, cols) for x in (d_zonal, d_merid, d_thick)]
    vmem = pl.BlockSpec(memory_space=pltpu.VMEM)
    hbm = pl.BlockSpec(memory_space=pltpu.HBM)
    params = pltpu.CompilerParams(vmem_limit_bytes=VMEM_BYTES)

    def call(kernel, name, out_shape, *operands, part=0.0):
        return pl.pallas_call(
            kernel,
            out_shape=out_shape,
            in_specs=[vmem] * len(operands),
            out_specs=jax.tree.map(lambda _: vmem, out_shape),
            compiler_params=params,
            cost_estimate=stage(part),
            name=name,
        )(*operands)

    def shape(*sizes):
        return jax.ShapeDtypeStruct(sizes, jnp.float32)

    full = shape(share * rows, cols)
    *east, small, island = pl.pallas_call(
        functools.partial(transport_kernel, -level_scale * row_scale, level_scale * line_scale),
        out_shape=(
            *[full] * n_dep,
            shape(n_dep, share + 8, cols),
            jax.ShapeDtypeStruct((rows, cols), jnp.int32),
        ),
        in_specs=[hbm] * 9,
        out_specs=tuple([vmem] * (n_dep + 2)),
        scratch_shapes=[pltpu.VMEM((deep, cols), jnp.float32)] * 3
        + [pltpu.VMEM((deep, cols), jnp.int32), pltpu.VMEM((rows, cols), jnp.int32)]
        + [pltpu.VMEM((dirs, deep, cols), jnp.bfloat16)] * 3
        + [
            pltpu.VMEM((dirs * rows, cols), jnp.float32),
            pltpu.SemaphoreType.DMA((6,)),
            pltpu.SemaphoreType.DMA((3, n_dep // 2)),
        ],
        compiler_params=params,
        name="transport",
    )(
        *(
            pltpu.with_memory_space_constraint(x, pltpu.HBM)
            for x in (*base, line_label, island_label, *moving)
        )
    )
    arrived = lax.ppermute(small, "lat", [(i, i ^ 1) for i in range(n_lat)])
    two = shape(2, share + 8, cols)
    near, far = call(core_kernel, "core", (two, two), small, arrived, part=PARTS[0])
    full = shape(share * (rows + 1), cols)
    half = shape(share + 8, cols)
    full = shape(share * (rows + 1), cols)
    twice = shape(2, share * (rows + 1), cols)
    large, leaving = call(blocks_kernel, "blocks", (twice, twice), arrived, *east)
    far, leaving = lax.optimization_barrier((far, leaving))
    leaving = lax.ppermute(leaving, "dep", [(i, i ^ 1) for i in range(n_dep)])
    own, out = call(far_kernel, "far", (half, half), near, swap(far, "dep", 1), part=PARTS[1])
    large, leaving = call(far_kernel, "halves", (full, full), large, leaving)
    leaving = lax.ppermute(leaving, "dep", [(i, i ^ 2) for i in range(n_dep)])
    small = call(add_kernel, "near", half, own, swap(out, "dep", 2), part=PARTS[2])
    before = []
    bit = 2
    while bit < n_lat:
        *before, small = call(
            functools.partial(lat_kernel, bit), "bands", (shape(share, cols), half),
            small, swap(small, "lat", bit), *before, part=PARTS[3],
        )
        bit *= 2
    bit = 1
    while 2 * bit < n_lon:
        small = small + swap(small, "lon", bit)
        bit *= 2
    small = call(add_kernel, "lines", half, small, swap(small, "lon", bit), part=PARTS[4])
    return call(
        stream_kernel, "stream", shape(share, rows, cols),
        large, leaving, *before, small, island,
    )


def solution(mesh):
    return jax.shard_map(
        shards,
        mesh=mesh,
        in_specs=(
            P("dep", "lat", "lon"),
            P("dep", "lat", "lon"),
            P("dep", "lat", "lon"),
            P(None, "dep", "lat", "lon"),
            P(None, "dep", "lat", "lon"),
            P(None, "dep", "lat", "lon"),
            P("dep", "lat", "lon"),
            P("lat", "lon"),
            P("lat", "lon"),
        ),
        out_specs=P("dep", "lat", "lon"),
        check_vma=False,
    )
```
